128 devices in a mesh: grp: 16 (over x, y), tp: 8 (over z, core).
Axes of the slice: x: 4, y: 4, z: 4, core: 2. Of those that a mesh axis runs over, the one named last changes fastest.
Arguments:
- hidden: bfloat16 [16384, 8192], P('grp'), may hold values from -300 to 300
- norm_gain: bfloat16 [8192], replicated, may hold values from 0.5 to 1.5
- w_query: bfloat16 [8192, 4096], P(None, 'tp'), may hold values from -0.0625 to 0.0625
- b_query: bfloat16 [4096], P('tp'), may hold values from -4 to 4
- w_key: bfloat16 [8192, 1024], P(None, 'tp'), may hold values from -0.0625 to 0.0625
- b_key: bfloat16 [1024], P('tp'), may hold values from -4 to 4
- w_value: bfloat16 [8192, 1024], P(None, 'tp'), may hold values from -0.0625 to 0.0625
- b_value: bfloat16 [1024], P('tp'), may hold values from -4 to 4
- kv_pool: bfloat16 [768, 64, 2048], P('grp', None, 'tp'), may hold values from -100 to 100
- page_table: int32 [256, 3], P('grp'), may hold values from 0 to 47, as said below
- prefix_len: int32 [256], P('grp'), may hold values from 0 to 192, as said below
- request_group: int32 [256, 1], replicated, may hold values from 0 to 15; in each aligned block of 16 rows (0 to 15, 16 to 31, ...) at most 2 rows name the same one
Outputs:
- attn_out: bfloat16 [16384, 4096], P('grp', 'tp')
- decode_pages: bfloat16 [2048, 64, 2048], P('grp', 'tp')
The draws below stay inside these ranges and needn't reach their ends.
Inputs may be any that keep to these rules, and one draw needn't show every extreme that they name: `request_group`: in the rows of one group (aligned blocks of 16 rows) each decode group is named at most 2 times. `prefix_len`: a multiple of 64. `page_table`: the rows of one group name each of its 48 pool pages once.
All inputs are finite; a program needn't handle non-finite values.
Results may differ from the reference program's by a relative error of at most 0.0076.
Values may be sent and summed in bfloat16 or wider, within the bound.
A program may use at most 192 MiB of HBM per device.

```python
import math
import jax
import jax.numpy as jnp
import numpy as np
from jax import lax

D = 8192
HEADS = 32
KVH = 8
HS = 128
PAGE = 64
PAIR_MOST = 2
REQ_DEV = 16
PREF_PG = 3
PP1 = 4
REQUESTS = 256
TOKENS = 16384
POOL = 48
POOL_ALL = 768
SLOTS = 32
KV_WIDTH = 2048
QW = 4096
N_GRP = 16


def draw_hidden(key, part):
    key = jax.random.fold_in(key, 11)
    key_rows, key_cols, key_vals = jax.random.split(key, 3)
    row_scale = jnp.exp(jax.random.uniform(key_rows, (TOKENS, 1), jnp.float32) * math.log(10.0))
    col_scale = jnp.exp(jax.random.uniform(key_cols, (1, D), jnp.float32) * math.log(10.0))
    values = jnp.clip(jax.random.normal(key_vals, (TOKENS, D), jnp.float32), -3.0, 3.0)
    return jnp.clip(values * row_scale * col_scale, -300.0, 300.0).astype(jnp.bfloat16)


def draw_kv_pool(key, part):
    key = jax.random.fold_in(key, 23)
    key_noise = jax.random.fold_in(key, 0)
    key_vals = jax.random.fold_in(key, 3)
    keys_part = jnp.clip(jax.random.normal(key_noise, (POOL_ALL, PAGE, KVH, HS), jnp.float32), -4.0, 4.0)
    vals_part = jnp.clip(jax.random.normal(key_vals, (POOL_ALL, PAGE, KVH, HS), jnp.float32), -4.0, 4.0)
    joined = jnp.concatenate([keys_part, vals_part], axis=3)
    return joined.reshape(POOL_ALL, PAGE, KV_WIDTH).astype(jnp.bfloat16)


def shuffle_pool(single):
    return jax.random.permutation(single, POOL)


def draw_page_table(key, part):
    key = jax.random.fold_in(key, 37)
    group_keys = jax.random.split(key, REQUESTS // REQ_DEV)
    orders = jax.vmap(shuffle_pool)(group_keys)
    return orders.reshape(REQUESTS, PREF_PG).astype(jnp.int32)


def draw_prefix_len(key, part):
    key = jax.random.fold_in(key, 41)
    key_len, key_top, key_gap = jax.random.split(key, 3)
    counts = jax.random.randint(key_len, (REQUESTS,), 0, PREF_PG + 1)
    longest = jax.random.randint(key_top, (), 0, REQUESTS)
    empty_one = (longest + 1 + jax.random.randint(key_gap, (), 0, REQUESTS - 1)) % REQUESTS
    indices = jnp.arange(REQUESTS)
    counts = jnp.where(indices == longest, PREF_PG, jnp.where(indices == empty_one, 0, counts))
    return (counts * PAGE).astype(jnp.int32)


def block_scale(rng, shape, cuts, low, largest):
    level = 1.0
    for dim, blocks in cuts:
        heights = jax.random.uniform(jax.random.fold_in(jax.random.fold_in(rng, 6), dim), (blocks,), jnp.float32, low / len(cuts), largest / len(cuts))
        level = level * jnp.repeat(jnp.exp(heights), shape[dim] // blocks).reshape((-1,) + (1,) * (len(shape) - 1 - dim))
    return level


def deal_out(key, own, number, rows, number_of, top, most, slope):
    ranking = jax.random.permutation(key, number_of)
    heavy_load, ordinary = portions_of(number_of, rows * top, most, slope, True), portions_of(number_of, rows * top, most, slope, False)
    places = jnp.arange(number_of)

    def named(tallies, turn):
        used = int((tallies > 0).sum())
        fixed = max(1, used // 4)
        passed = fixed + (places - fixed + turn * (used - fixed)) % max(1, number_of - fixed)
        return jnp.zeros((number_of,), jnp.int32).at[ranking[jnp.where(places < fixed, places, passed)]].set(jnp.asarray(tallies, jnp.int32))

    tallies = jnp.where(number % 4 == 0, named(heavy_load, number // 4), named(ordinary, number - number // 4 - 1))
    mixed = jax.random.permutation(jax.random.fold_in(own, 3), number_of)
    giver, sink = mixed[0:number_of // 2 * 2:2], mixed[1:number_of // 2 * 2:2]
    room = jnp.minimum(tallies[giver] - 1, most - tallies[sink]) // 2
    room = jnp.where((giver == ranking[0]) | (sink == ranking[0]) | (tallies[sink] == 0), 0, jnp.maximum(room, 0))
    passed = jax.random.randint(jax.random.fold_in(own, 4), (number_of // 2,), 0, 1 << 20) % (room + 1)
    tallies = tallies.at[giver].add(-passed).at[sink].add(passed)
    labels = jnp.searchsorted(jnp.cumsum(tallies), jnp.arange(rows * top), side="right").astype(jnp.int32)
    grid = labels.reshape(top, rows).T
    grid = grid[jax.random.permutation(jax.random.fold_in(own, 1), rows)]
    turn = jax.random.randint(jax.random.fold_in(own, 2), (rows, 1), 0, top)
    return jnp.take_along_axis(grid, (jnp.arange(top)[None, :] + turn) % top, axis=1)


def portions_of(amount, total, limit, lean, full):
    loads = [(1 << 20) // math.isqrt(standing ** lean) + 1 for standing in range(1, amount + 1)]
    largest = limit if full else min(limit, max(-(-total // amount), total * loads[0] // sum(loads)))
    least = 1 if total - largest >= amount - 1 else 0
    holding, surplus = [largest] + [least] * (amount - 1), total - largest - least * (amount - 1)
    while surplus > 0:
        free = [i for i in range(1, amount) if holding[i] < largest] or [i for i in range(1, amount) if holding[i] < limit]
        pool, remaining = sum([loads[i] for i in free]), surplus
        for i in free:
            addition = min(limit - holding[i], max(1, remaining * loads[i] // pool), surplus)
            holding[i] = holding[i] + addition
            surplus = surplus - addition
    return np.array(holding)


def bell_draw(stream_key, dims, spread, most, pieces=(), kind=jnp.bfloat16):
    values = spread * jax.random.normal(stream_key, dims, jnp.float32)
    if pieces:
        values = values * block_scale(stream_key, dims, pieces, -0.22, 0.18)
    return jnp.clip(values, -most, most).astype(kind)


def setup_inputs(seed: int = 0) -> dict:
    key_list = jax.random.split(jax.random.key(seed), 13)
    hidden = draw_hidden(jax.random.fold_in(key_list[12], 71), 0)
    norm_gain = jnp.clip(jax.random.uniform(key_list[1], (D,), jnp.float32, 0.5, 1.5), 0.5, 1.5).astype(jnp.bfloat16)
    w_query = bell_draw(key_list[2], (D, QW), D ** -0.5, 0.0625, ((1, 8),))
    b_query = bell_draw(key_list[3], (QW,), 1.0, 4.0, ((0, 8),))
    w_key = bell_draw(key_list[4], (D, KVH * HS), D ** -0.5, 0.0625, ((1, 8),))
    b_key = bell_draw(key_list[5], (KVH * HS,), 1.0, 4.0, ((0, 8),))
    w_value = bell_draw(key_list[6], (D, KVH * HS), D ** -0.5, 0.0625, ((1, 8),))
    b_value = bell_draw(key_list[7], (KVH * HS,), 1.0, 4.0, ((0, 8),))
    kv_pool = draw_kv_pool(jax.random.fold_in(key_list[12], 71), 0)
    page_table = draw_page_table(jax.random.fold_in(key_list[12], 71), 0)
    prefix_len = draw_prefix_len(jax.random.fold_in(key_list[12], 71), 0)
    request_group_keys = jax.random.split(jax.random.fold_in(key_list[11], 1), REQUESTS // REQ_DEV)
    request_group_turns = jax.random.permutation(jax.random.fold_in(key_list[11], 3), REQUESTS // REQ_DEV)
    request_group = jax.vmap(lambda own, number: deal_out(jax.random.fold_in(key_list[11], 2), own, number, REQ_DEV, N_GRP, 1, PAIR_MOST, 2))(request_group_keys, request_group_turns).reshape((REQUESTS, 1))
    return {"hidden": hidden, "norm_gain": norm_gain, "w_query": w_query, "b_query": b_query, "w_key": w_key, "b_key": b_key, "w_value": w_value, "b_value": b_value, "kv_pool": kv_pool, "page_table": page_table, "prefix_len": prefix_len, "request_group": request_group}


rope_base = 1000000.0
norm_eps = 1e-06

def rotate(values, positions):
    half_size = values.shape[-1] // 2
    inverse = rope_base ** (-(jnp.arange(half_size, dtype=jnp.float32) * 2.0) / (2 * half_size))
    angles = positions.astype(jnp.float32)[:, :, None] * inverse[None, None, :]
    cosine = jnp.cos(angles)[:, :, None, :]
    sine_part = jnp.sin(angles)[:, :, None, :]
    first = values[..., :half_size]
    second = values[..., half_size:]
    return jnp.concatenate([first * cosine - second * sine_part, second * cosine + first * sine_part], axis=-1)

def rank_within(targets, owners):
    count = targets.shape[0]
    order = jnp.arange(count, dtype=jnp.int32)
    before = (order[None, :] < order[:, None]) & (owners[None, :] == owners[:, None]) & (targets[None, :] == targets[:, None])
    return lax.optimization_barrier(jnp.sum(before.astype(jnp.int32), axis=1)).astype(jnp.int32)

def reference(hidden, norm_gain, w_query, b_query, w_key, b_key, w_value, b_value, kv_pool, page_table, prefix_len, request_group):
    widened = hidden.astype(jnp.float32)
    inv_rms = lax.rsqrt(lax.optimization_barrier(jnp.mean(widened * widened, axis=1, keepdims=True)) + norm_eps)
    normed = (widened * inv_rms * norm_gain.astype(jnp.float32)).astype(jnp.bfloat16)
    query = jnp.dot(normed, w_query, preferred_element_type=jnp.float32) + b_query.astype(jnp.float32)
    keys_new = jnp.dot(normed, w_key, preferred_element_type=jnp.float32) + b_key.astype(jnp.float32)
    values_new = jnp.dot(normed, w_value, preferred_element_type=jnp.float32) + b_value.astype(jnp.float32)
    positions = prefix_len[:, None] + jnp.arange(PAGE, dtype=jnp.int32)[None, :]
    query_rot = rotate(query.reshape(REQUESTS, PAGE, HEADS, HS), positions).astype(jnp.bfloat16)
    key_rot = rotate(keys_new.reshape(REQUESTS, PAGE, KVH, HS), positions).astype(jnp.bfloat16)
    value_store = values_new.reshape(REQUESTS, PAGE, KVH, HS).astype(jnp.bfloat16)
    new_page = jnp.concatenate([key_rot, value_store], axis=3).reshape(REQUESTS, PAGE, KV_WIDTH)
    prefix_pages = prefix_len // PAGE
    owners = jnp.arange(REQUESTS, dtype=jnp.int32) // REQ_DEV
    page_ids = jnp.arange(PP1, dtype=jnp.int32)[None, :]
    earlier = kv_pool[(owners[:, None] * POOL + page_table).astype(jnp.int32)]
    earlier = jnp.where((page_ids[:, :-1] < prefix_pages[:, None])[:, :, None, None], earlier, jnp.zeros_like(earlier))
    padded = jnp.concatenate([earlier, jnp.zeros_like(earlier[:, :1])], axis=1)
    request_pages = jnp.where((page_ids == prefix_pages[:, None])[:, :, None, None], new_page[:, None], padded)

    def attend(operands):
        query_one, pages_one, position_one = operands
        flattened = pages_one.reshape(PP1 * PAGE, KVH, 2 * HS).astype(jnp.float32)
        grouped = query_one.reshape(PAGE, KVH, HEADS // KVH, HS).astype(jnp.float32)
        scores = jnp.einsum('qkgd,skd->kgqs', grouped, flattened[..., :HS]) * (1.0 / math.sqrt(HS))
        visible = jnp.arange(PP1 * PAGE, dtype=jnp.int32)[None, :] <= position_one[:, None]
        scores = jnp.where(visible[None, None], scores, -1e+30)
        highest = lax.optimization_barrier(jnp.max(scores, axis=-1, keepdims=True))
        weights = jnp.exp(scores - highest)
        shares = (weights / lax.optimization_barrier(jnp.sum(weights, axis=-1, keepdims=True))).astype(jnp.bfloat16)
        blended = jnp.einsum('kgqs,skd->qkgd', shares.astype(jnp.float32), flattened[..., HS:])
        return blended.reshape(PAGE, HEADS * HS).astype(jnp.bfloat16)
    attn_out = lax.map(attend, (query_rot, request_pages, positions)).reshape(TOKENS, QW)
    targets = request_group[:, 0]
    order_rank = rank_within(targets, owners)
    slot_ids = (targets * SLOTS + owners * PAIR_MOST + order_rank).astype(jnp.int32)
    placed = jnp.zeros((N_GRP * SLOTS, PP1, PAGE, KV_WIDTH), jnp.bfloat16).at[slot_ids].set(request_pages)
    decode_pages = placed.reshape(N_GRP * SLOTS * PP1, PAGE, KV_WIDTH)
    return (attn_out, decode_pages)
```

```python
import functools
import math

import jax
import jax.numpy as jnp
import numpy as np
from jax import lax
from jax.experimental import pallas as pl
from jax.experimental.pallas import tpu as pltpu
from jax.sharding import PartitionSpec as P

HS = 128
PAGE = 64
PAIR = 2
GX = 4
GY = 4
GRP = 16
TP = 8
PG = 3
ROPE_BASE = 1000000.0
EPS = 1e-06
MESH = pl.DeviceIdType.MESH
RB = 256
KC = 1024


def rope_tables():
    half = HS // 2
    inverse = np.float32(ROPE_BASE) ** (
        -(np.arange(half, dtype=np.float32) * np.float32(2.0)) / np.float32(HS)
    )
    positions = np.arange((PG + 1) * PAGE, dtype=np.float32)
    angles = (positions[:, None] * inverse.astype(np.float32)[None, :]).astype(np.float32)
    cosine = np.cos(angles.astype(np.float64)).astype(np.float32)
    sine = np.sin(angles.astype(np.float64)).astype(np.float32)
    shape = (PG + 1, PAGE, HS)
    return (
        np.concatenate([cosine, cosine], axis=1).reshape(shape),
        np.concatenate([-sine, sine], axis=1).reshape(shape),
    )


def grp_at(g, i):
    x, y = g // GY, lax.rem(g, GY)
    return lax.rem(x + i // GY, GX) * GY + lax.rem(y + lax.rem(i, GY), GY)


def grp_back(g, i):
    x, y = g // GY, lax.rem(g, GY)
    return lax.rem(x + GX - i // GY, GX) * GY + lax.rem(y + GY - lax.rem(i, GY), GY)


def main_kernel(
    hidden,
    gain,
    w_query,
    b_query,
    w_key,
    b_key,
    w_value,
    b_value,
    pool,
    cos_ref,
    sin_ref,
    page_table,
    prefix_len,
    request_group,
    attn,
    cached,
    fresh,
    meta,
    hid,
    wq,
    wkv,
    poolv,
    ss,
    acc,
    newkv,
    qrot,
    attnv,
    send_a,
    recv_a,
    zsend_b,
    zrecv_b,
    zsend_n,
    zrecv_n,
    send_b,
    send_n,
    send_m,
    table,
    load_sem,
    own_sem,
    a_ss,
    a_rs,
    b_ss,
    b_rs,
    n_ss,
    n_rs,
    m_ss,
    m_rs,
    za_ss,
    za_rs,
    zb_ss,
    zb_rs,
    zn_ss,
    zn_rs,
):
    g = lax.axis_index("grp")
    t = lax.axis_index("tp")
    rows, width = hid.shape
    requests = rows // PAGE
    blocks = rows // RB
    steps = width // KC
    per_block = RB // PAGE
    kvw = 2 * HS

    def cols(who):
        return pl.ds(pl.multiple_of(who * kvw, kvw), kvw)

    loads = [
        pltpu.make_async_copy(pool, poolv, load_sem.at[0]),
        pltpu.make_async_copy(w_key, wkv.at[:, 0:HS], load_sem.at[1]),
        pltpu.make_async_copy(w_value, wkv.at[:, HS : 2 * HS], load_sem.at[2]),
    ]
    for b in range(blocks):
        part = pl.ds(b * RB, RB)
        loads.append(pltpu.make_async_copy(hidden.at[part], hid.at[part], load_sem.at[4 + b]))
    loads.append(pltpu.make_async_copy(w_query, wq, load_sem.at[3]))

    barrier = pltpu.get_barrier_semaphore()

    def greet_grp(i, _):
        pl.semaphore_signal(barrier, inc=1, device_id=(grp_at(g, i), t), device_id_type=MESH)
        return 0

    def greet_tp(i, _):
        pl.semaphore_signal(barrier, inc=1, device_id=(g, lax.rem(t + i, TP)), device_id_type=MESH)
        return 0

    lax.fori_loop(1, GRP, greet_grp, 0)
    lax.fori_loop(1, TP, greet_tp, 0)
    for load in loads:
        load.start()

    def find(d, _):
        first = jnp.int32(requests)
        second = jnp.int32(requests)
        for j in range(requests - 1, -1, -1):
            hit = request_group[g * requests + j] == d
            second = jnp.where(hit, first, second)
            first = jnp.where(hit, jnp.int32(j), first)
        table[2 * d] = first
        table[2 * d + 1] = second
        return 0

    lax.fori_loop(0, GRP, find, 0)

    def slot_of(slot):
        j = table[slot]
        used = j < requests
        jc = jnp.minimum(j, requests - 1)
        n = jnp.where(used, prefix_len[jc] // PAGE, 0)
        return used, jc, n

    loads[0].wait()

    def pack_a(slot, _):
        used, jc, n = slot_of(slot)
        page = poolv[page_table[jc * PG]]
        send_a[slot] = jnp.where(n > 0, page, jnp.zeros_like(page))
        return 0

    lax.fori_loop(0, PAIR * GRP, pack_a, 0)

    def pack_zb(j, _):
        for p in range(1, PG):
            zsend_b[(p - 1) * requests + j] = poolv[page_table[j * PG + p]]
        return 0

    lax.fori_loop(0, requests, pack_zb, 0)

    def pack_m(d, _):
        _, _, n0 = slot_of(2 * d)
        _, _, n1 = slot_of(2 * d + 1)
        row = lax.broadcasted_iota(jnp.int32, (8, 128), 0)
        send_m[d] = jnp.where(row == 0, n0, n1)
        return 0

    lax.fori_loop(0, GRP, pack_m, 0)

    pl.semaphore_wait(barrier, GRP - 1 + TP - 1)

    def two(who):
        return pl.ds(PAIR * who, PAIR)

    def copy_a(i, who):
        d = grp_at(g, i)
        return pltpu.make_async_remote_copy(
            src_ref=send_a.at[two(d)], dst_ref=recv_a.at[two(who)],
            send_sem=a_ss.at[i], recv_sem=a_rs.at[i], device_id=(d, t), device_id_type=MESH,
        )

    def copy_b(i, who):
        d = grp_at(g, i)
        return pltpu.make_async_remote_copy(
            src_ref=send_b.at[two(d)], dst_ref=cached.at[two(who), pl.ds(1, PG - 1)],
            send_sem=b_ss.at[i], recv_sem=b_rs.at[i], device_id=(d, t), device_id_type=MESH,
        )

    def copy_n(i, who):
        d = grp_at(g, i)
        return pltpu.make_async_remote_copy(
            src_ref=send_n.at[two(d)], dst_ref=fresh.at[two(who)],
            send_sem=n_ss.at[i], recv_sem=n_rs.at[i], device_id=(d, t), device_id_type=MESH,
        )

    def copy_m(i, who):
        d = grp_at(g, i)
        return pltpu.make_async_remote_copy(
            src_ref=send_m.at[d], dst_ref=meta.at[who],
            send_sem=m_ss.at[i], recv_sem=m_rs.at[i], device_id=(d, t), device_id_type=MESH,
        )

    def copy_za(i, who):
        u = lax.rem(t + i, TP)
        return pltpu.make_async_remote_copy(
            src_ref=recv_a.at[:, u], dst_ref=cached.at[:, 0, :, cols(who)],
            send_sem=za_ss.at[i], recv_sem=za_rs.at[i], device_id=(g, u), device_id_type=MESH,
        )

    def copy_zb(i, who):
        u = lax.rem(t + i, TP)
        return pltpu.make_async_remote_copy(
            src_ref=zsend_b.at[:, u], dst_ref=zrecv_b.at[:, :, cols(who)],
            send_sem=zb_ss.at[i], recv_sem=zb_rs.at[i], device_id=(g, u), device_id_type=MESH,
        )

    def copy_zn(i, who):
        u = lax.rem(t + i, TP)
        return pltpu.make_async_remote_copy(
            src_ref=zsend_n.at[:, u], dst_ref=zrecv_n.at[:, :, cols(who)],
            send_sem=zn_ss.at[i], recv_sem=zn_rs.at[i], device_id=(g, u), device_id_type=MESH,
        )

    def each(count, copy, me, action):
        def step(i, _):
            made = copy(i, me(i))
            getattr(made, action)()
            return 0

        lax.fori_loop(1, count, step, 0)

    def start_grp(copy):
        each(GRP, copy, lambda i: g, "start")

    def start_tp(copy):
        each(TP, copy, lambda i: t, "start")

    def arrived_grp(copy):
        each(GRP, copy, lambda i: grp_back(g, i), "wait_recv")

    def arrived_tp(copy):
        each(TP, copy, lambda i: lax.rem(t + TP - i, TP), "wait_recv")

    def sent_grp(copy):
        each(GRP, copy, lambda i: g, "wait_send")

    def sent_tp(copy):
        each(TP, copy, lambda i: t, "wait_send")

    own_a = pltpu.make_async_copy(send_a.at[two(g)], recv_a.at[two(g)], own_sem.at[0])
    own_zb = pltpu.make_async_copy(zsend_b.at[:, t], zrecv_b.at[:, :, cols(t)], own_sem.at[1])
    own_zn = pltpu.make_async_copy(zsend_n.at[:, t], zrecv_n.at[:, :, cols(t)], own_sem.at[2])
    own_b = pltpu.make_async_copy(
        send_b.at[two(g)], cached.at[two(g), pl.ds(1, PG - 1)], own_sem.at[3]
    )
    own_n = pltpu.make_async_copy(send_n.at[two(g)], fresh.at[two(g)], own_sem.at[4])
    own_m = pltpu.make_async_copy(send_m.at[g], meta.at[g], own_sem.at[5])
    own_za = pltpu.make_async_copy(recv_a.at[:, t], cached.at[:, 0, :, cols(t)], own_sem.at[6])
    attn_copy = pltpu.make_async_copy(attnv, attn, own_sem.at[7])

    start_tp(copy_zb)
    start_grp(copy_a)
    own_zb.start()
    own_a.start()
    start_grp(copy_m)
    own_m.start()

    loads[1].wait()
    loads[2].wait()
    for b in range(blocks):
        loads[3 + b].wait()

    def rotated(values, n):
        return values * cos_ref[n] + pltpu.roll(values, HS // 2, 1) * sin_ref[n]

    def kv_block(b, _):
        part = pl.ds(pl.multiple_of(b * RB, RB), RB)
        ss[part, :] = jnp.zeros((RB, HS), jnp.float32)
        acc[:, 0:kvw] = jnp.zeros((RB, kvw), jnp.float32)

        def step(c, _):
            deep = pl.ds(pl.multiple_of(c * KC, KC), KC)
            x = hid[part, deep]
            xf = x.astype(jnp.float32)
            total = ss[part, :]
            for k in range(KC // HS):
                piece = xf[:, k * HS : (k + 1) * HS]
                total = total + piece * piece
            ss[part, :] = total
            xg = x * gain[:, deep]
            hid[part, deep] = xg
            acc[:, 0:kvw] += jnp.dot(xg, wkv[deep, :], preferred_element_type=jnp.float32)
            return 0

        lax.fori_loop(0, steps, step, 0)
        scale = lax.rsqrt(jnp.sum(ss[part, :], axis=1, keepdims=True) / width + EPS)
        ss[part, :] = jnp.broadcast_to(scale, (RB, HS))
        keys = acc[:, 0:HS] * scale + b_key[...].astype(jnp.float32)
        values = acc[:, HS:kvw] * scale + b_value[...].astype(jnp.float32)
        for r in range(per_block):
            j = b * per_block + r
            n = prefix_len[j] // PAGE
            span = slice(r * PAGE, (r + 1) * PAGE)
            joined = jnp.concatenate([rotated(keys[span], n), values[span]], axis=1)
            newkv[j] = joined.astype(jnp.bfloat16)
            zsend_n[j] = joined.reshape(TP, PAGE // TP, kvw).astype(jnp.bfloat16)
        return 0

    lax.fori_loop(0, blocks, kv_block, 0)
    start_tp(copy_zn)
    own_zn.start()

    arrived_tp(copy_zb)
    own_zb.wait()

    def pack_b(slot, _):
        used, jc, n = slot_of(slot)
        for p in range(1, PG):
            page = zrecv_b[(p - 1) * requests + jc]
            send_b[slot, p - 1] = jnp.where(n > p, page, jnp.zeros_like(page))
        return 0

    lax.fori_loop(0, PAIR * GRP, pack_b, 0)
    start_grp(copy_b)
    own_b.start()

    arrived_grp(copy_a)
    own_a.wait()
    start_tp(copy_za)
    own_za.start()

    loads[3 + blocks].wait()

    def q_block(b, _):
        part = pl.ds(pl.multiple_of(b * RB, RB), RB)
        acc[...] = jnp.zeros(acc.shape, jnp.float32)

        def step(c, _):
            deep = pl.ds(pl.multiple_of(c * KC, KC), KC)
            acc[...] += jnp.dot(hid[part, deep], wq[deep, :], preferred_element_type=jnp.float32)
            return 0

        lax.fori_loop(0, steps, step, 0)
        scale = ss[part, :]
        for h in range(wq.shape[1] // HS):
            lanes = slice(h * HS, (h + 1) * HS)
            one = acc[:, lanes] * scale + b_query[:, lanes].astype(jnp.float32)
            for r in range(per_block):
                j = b * per_block + r
                n = prefix_len[j] // PAGE
                turned = rotated(one[r * PAGE : (r + 1) * PAGE], n)
                qrot[j, h * PAGE : (h + 1) * PAGE, :] = turned.astype(jnp.bfloat16)
        return 0

    lax.fori_loop(0, blocks, q_block, 0)

    arrived_tp(copy_zn)
    own_zn.wait()

    def pack_n(slot, _):
        used, jc, n = slot_of(slot)
        page = zrecv_n[jc]
        send_n[slot] = jnp.where(used, page, jnp.zeros_like(page))
        return 0

    lax.fori_loop(0, PAIR * GRP, pack_n, 0)
    start_grp(copy_n)
    own_n.start()

    heads = wq.shape[1] // HS
    qrows = heads * PAGE
    length = (PG + 1) * PAGE

    def attend(j, _):
        n = prefix_len[j] // PAGE
        pages = [poolv[page_table[j * PG + p]].reshape(PAGE, kvw) for p in range(PG)]
        pages.append(newkv[j])
        kv = jnp.concatenate(pages, axis=0)
        scores = lax.dot_general(
            qrot[j], kv[:, 0:HS], (((1,), (1,)), ((), ())), preferred_element_type=jnp.float32
        ) * (1.0 / math.sqrt(HS))
        column = lax.broadcasted_iota(jnp.int32, (qrows, length), 1)
        token = lax.rem(lax.broadcasted_iota(jnp.int32, (qrows, length), 0), PAGE)
        limit = jnp.where(column < PG * PAGE, n * PAGE, token + (PG * PAGE + 1))
        scores = jnp.where(column < limit, scores, -1e30)
        highest = jnp.max(scores, axis=1, keepdims=True)
        weights = jnp.exp(scores - highest)
        total = jnp.sum(weights, axis=1, keepdims=True)
        out = jnp.dot(weights.astype(jnp.bfloat16), kv[:, HS:kvw], preferred_element_type=jnp.float32)
        out = (out / total).astype(jnp.bfloat16)
        span = pl.ds(pl.multiple_of(j * PAGE, PAGE), PAGE)
        for h in range(heads):
            attnv[span, h * HS : (h + 1) * HS] = out[h * PAGE : (h + 1) * PAGE]
        return 0

    lax.fori_loop(0, requests, attend, 0)
    attn_copy.start()

    arrived_grp(copy_m)
    arrived_tp(copy_za)
    arrived_grp(copy_b)
    arrived_grp(copy_n)
    for own in (own_za, own_b, own_n, own_m, attn_copy):
        own.wait()
    sent_tp(copy_zb)
    sent_grp(copy_a)
    sent_grp(copy_m)
    sent_tp(copy_zn)
    sent_grp(copy_b)
    sent_tp(copy_za)
    sent_grp(copy_n)


def place_kernel(meta, cached, fresh, out):
    slots = fresh.shape[0]
    for slot in range(slots):
        out[slot, 0:PG] = cached[slot]
        out[slot, PG] = jnp.zeros(fresh.shape[1:], out.dtype)
        out[slot, meta[slot // PAIR, slot % PAIR, 0]] = fresh[slot]


def local(
    hidden, norm_gain, w_query, b_query, w_key, b_key, w_value, b_value,
    kv_pool, page_table, prefix_len, request_group,
):
    rows, width = hidden.shape
    qw = w_query.shape[1]
    requests = prefix_len.shape[0]
    npool = kv_pool.shape[0]
    kvw = kv_pool.shape[2]
    page_rows = PAGE // TP
    full = TP * kvw
    slots = PAIR * GRP
    bf = jnp.bfloat16
    cosine, sine = rope_tables()
    any_ = pl.BlockSpec(memory_space=pl.ANY)
    vmem = pl.BlockSpec(memory_space=pltpu.VMEM)
    smem = pl.BlockSpec(memory_space=pltpu.SMEM)
    dma = pltpu.SemaphoreType.DMA
    attn, cached, fresh, meta = pl.pallas_call(
        main_kernel,
        name="span_and_routes",
        out_shape=[
            jax.ShapeDtypeStruct((rows, qw), bf),
            jax.ShapeDtypeStruct((slots, PG, page_rows, full), bf),
            jax.ShapeDtypeStruct((slots, page_rows, full), bf),
            jax.ShapeDtypeStruct((GRP, 8, 128), jnp.int32),
        ],
        in_specs=[any_, vmem, any_, vmem, any_, vmem, any_, vmem, any_, vmem, vmem, smem, smem, smem],
        out_specs=[any_, any_, any_, any_],
        scratch_shapes=[
            pltpu.VMEM((rows, width), bf),
            pltpu.VMEM((width, qw), bf),
            pltpu.VMEM((width, 2 * HS), bf),
            pltpu.VMEM((npool, TP, page_rows, kvw), bf),
            pltpu.VMEM((rows, HS), jnp.float32),
            pltpu.VMEM((RB, qw), jnp.float32),
            pltpu.VMEM((requests, PAGE, kvw), bf),
            pltpu.VMEM((requests, qw // HS * PAGE, HS), bf),
            pltpu.VMEM((rows, qw), bf),
            pltpu.VMEM((slots, TP, page_rows, kvw), bf),
            pltpu.VMEM((slots, TP, page_rows, kvw), bf),
            pltpu.VMEM(((PG - 1) * requests, TP, page_rows, kvw), bf),
            pltpu.VMEM(((PG - 1) * requests, page_rows, full), bf),
            pltpu.VMEM((requests, TP, page_rows, kvw), bf),
            pltpu.VMEM((requests, page_rows, full), bf),
            pltpu.VMEM((slots, PG - 1, page_rows, full), bf),
            pltpu.VMEM((slots, page_rows, full), bf),
            pltpu.VMEM((GRP, 8, 128), jnp.int32),
            pltpu.SMEM((slots,), jnp.int32),
            dma((4 + rows // RB,)),
            dma((8,)),
            dma((GRP,)), dma((GRP,)),
            dma((GRP,)), dma((GRP,)),
            dma((GRP,)), dma((GRP,)),
            dma((GRP,)), dma((GRP,)),
            dma((TP,)), dma((TP,)),
            dma((TP,)), dma((TP,)),
            dma((TP,)), dma((TP,)),
        ],
        cost_estimate=pl.CostEstimate(
            flops=2 * rows * width * (qw + 2 * HS), bytes_accessed=40 << 20, transcendentals=0
        ),
        compiler_params=pltpu.CompilerParams(
            collective_id=0, has_side_effects=True, vmem_limit_bytes=58 << 20
        ),
    )(
        hidden,
        norm_gain.reshape(1, width),
        w_query,
        b_query.reshape(1, qw),
        w_key,
        b_key.reshape(1, HS),
        w_value,
        b_value.reshape(1, HS),
        kv_pool.reshape(npool, TP, page_rows, kvw),
        jnp.asarray(cosine),
        jnp.asarray(sine),
        page_table.reshape(-1),
        prefix_len,
        request_group.reshape(-1),
    )
    steps = 4
    part = slots // steps
    pages = pl.pallas_call(
        place_kernel,
        name="place_new_pages",
        grid=(steps,),
        out_shape=jax.ShapeDtypeStruct((slots, PG + 1, page_rows, full), bf),
        in_specs=[
            pl.BlockSpec((part // PAIR, 8, 128), lambda i: (i, 0, 0), memory_space=pltpu.SMEM),
            pl.BlockSpec((part, PG, page_rows, full), lambda i: (i, 0, 0, 0)),
            pl.BlockSpec((part, page_rows, full), lambda i: (i, 0, 0)),
        ],
        out_specs=pl.BlockSpec((part, PG + 1, page_rows, full), lambda i: (i, 0, 0, 0)),
        compiler_params=pltpu.CompilerParams(vmem_limit_bytes=32 << 20),
    )(meta, cached, fresh)
    return attn, pages.reshape(slots * (PG + 1), page_rows, full)


def solution(mesh):
    in_specs = (
        P("grp", None),
        P(),
        P(None, "tp"),
        P("tp"),
        P(None, "tp"),
        P("tp"),
        P(None, "tp"),
        P("tp"),
        P("grp", None, "tp"),
        P("grp", None),
        P("grp"),
        P(),
    )
    out_specs = (P("grp", "tp"), P("grp", "tp", None))
    return jax.shard_map(local, mesh=mesh, in_specs=in_specs, out_specs=out_specs, check_vma=False)
```

```python
import functools
import math

import jax
import jax.numpy as jnp
import numpy as np
from jax import lax
from jax.experimental import pallas as pl
from jax.experimental.pallas import tpu as pltpu
from jax.sharding import PartitionSpec as P

HS = 128
PAGE = 64
PAIR = 2
GX = 4
GY = 4
GRP = 16
TP = 8
PG = 3
ROPE_BASE = 1000000.0
EPS = 1e-06
MESH = pl.DeviceIdType.MESH
RB = 256
KC = 1024


def rope_tables():
    half = HS // 2
    inverse = np.float32(ROPE_BASE) ** (
        -(np.arange(half, dtype=np.float32) * np.float32(2.0)) / np.float32(HS)
    )
    positions = np.arange((PG + 1) * PAGE, dtype=np.float32)
    angles = (positions[:, None] * inverse.astype(np.float32)[None, :]).astype(np.float32)
    cosine = np.cos(angles.astype(np.float64)).astype(np.float32)
    sine = np.sin(angles.astype(np.float64)).astype(np.float32)
    shape = (PG + 1, PAGE, HS)
    return (
        np.concatenate([cosine, cosine], axis=1).reshape(shape),
        np.concatenate([-sine, sine], axis=1).reshape(shape),
    )


ORDER = (
    (2, 2), (0, 1), (1, 0), (2, 1), (1, 2), (0, 3), (3, 0), (2, 3),
    (3, 2), (1, 1), (3, 3), (0, 2), (2, 0), (1, 3), (3, 1),
)


def grp_at(g, i):
    x, y = g // GY, lax.rem(g, GY)
    dx, dy = ORDER[i - 1]
    return lax.rem(x + dx, GX) * GY + lax.rem(y + dy, GY)


def grp_back(g, i):
    x, y = g // GY, lax.rem(g, GY)
    dx, dy = ORDER[i - 1]
    return lax.rem(x + GX - dx, GX) * GY + lax.rem(y + GY - dy, GY)


def main_kernel(
    hidden,
    gain,
    w_query,
    b_query,
    w_key,
    b_key,
    w_value,
    b_value,
    pool,
    cos_ref,
    sin_ref,
    page_table,
    prefix_len,
    request_group,
    attnv,
    pages,
    hid,
    wq,
    wkv,
    poolv,
    ss,
    acc,
    newkv,
    qrot,
    fresh,
    metav,
    metas,
    gains,
    send_a,
    recv_a,
    zsend_b,
    zrecv_b,
    zsend_n,
    zrecv_n,
    send_b,
    send_n,
    send_m,
    table,
    load_sem,
    own_sem,
    a_ss,
    a_rs,
    b_ss,
    b_rs,
    n_ss,
    n_rs,
    m_ss,
    m_rs,
    za_ss,
    za_rs,
    zb_ss,
    zb_rs,
    zn_ss,
    zn_rs,
):
    g = lax.axis_index("grp")
    t = lax.axis_index("tp")
    rows, width = hid.shape
    requests = rows // PAGE
    blocks = rows // RB
    steps = width // KC
    per_block = RB // PAGE
    kvw = 2 * HS

    def cols(who):
        return pl.ds(pl.multiple_of(who * kvw, kvw), kvw)

    loads = [
        pltpu.make_async_copy(pool, poolv, load_sem.at[0]),
        pltpu.make_async_copy(w_key, wkv.at[:, 0:HS], load_sem.at[1]),
        pltpu.make_async_copy(w_value, wkv.at[:, HS : 2 * HS], load_sem.at[2]),
    ]
    for b in range(blocks):
        part = pl.ds(b * RB, RB)
        loads.append(pltpu.make_async_copy(hidden.at[part], hid.at[part], load_sem.at[4 + b]))
    loads.append(pltpu.make_async_copy(w_query, wq, load_sem.at[3]))

    barrier = pltpu.get_barrier_semaphore()

    for i in range(1, GRP):
        pl.semaphore_signal(barrier, inc=1, device_id=(grp_at(g, i), t), device_id_type=MESH)
    for i in range(1, TP):
        pl.semaphore_signal(barrier, inc=1, device_id=(g, lax.rem(t + i, TP)), device_id_type=MESH)
    for load in loads:
        load.start()

    def find(d, _):
        first = jnp.int32(requests)
        second = jnp.int32(requests)
        for j in range(requests - 1, -1, -1):
            hit = request_group[g * requests + j] == d
            second = jnp.where(hit, first, second)
            first = jnp.where(hit, jnp.int32(j), first)
        table[2 * d] = first
        table[2 * d + 1] = second
        return 0

    lax.fori_loop(0, GRP, find, 0)

    def slot_of(slot):
        j = table[slot]
        used = j < requests
        jc = jnp.minimum(j, requests - 1)
        n = jnp.where(used, prefix_len[jc] // PAGE, -1)
        return used, jc, n

    loads[0].wait()

    def pack_a(d, _):
        for k in range(PAIR):
            slot = PAIR * d + k
            used, jc, n = slot_of(slot)
            page = poolv[page_table[0, jc]]
            send_a[slot] = jnp.where(n > 0, page, jnp.zeros_like(page))
        return 0

    lax.fori_loop(0, GRP, pack_a, 0)

    def pack_zb(j, _):
        for p in range(1, PG):
            zsend_b[(p - 1) * requests + j] = poolv[page_table[p, j]]
        return 0

    lax.fori_loop(0, requests, pack_zb, 0)

    pl.semaphore_wait(barrier, GRP - 1 + TP - 1)

    def two(who):
        return pl.ds(PAIR * who, PAIR)

    def copy_a(i, who):
        d = grp_at(g, i)
        return pltpu.make_async_remote_copy(
            src_ref=send_a.at[two(d)], dst_ref=recv_a.at[two(who)],
            send_sem=a_ss.at[i], recv_sem=a_rs.at[i], device_id=(d, t), device_id_type=MESH,
        )

    def copy_b(i, who):
        d = grp_at(g, i)
        return pltpu.make_async_remote_copy(
            src_ref=send_b.at[two(d)], dst_ref=pages.at[two(who), pl.ds(1, PG - 1)],
            send_sem=b_ss.at[i], recv_sem=b_rs.at[i], device_id=(d, t), device_id_type=MESH,
        )

    def copy_n(i, who):
        d = grp_at(g, i)
        return pltpu.make_async_remote_copy(
            src_ref=send_n.at[two(d)], dst_ref=fresh.at[two(who)],
            send_sem=n_ss.at[i], recv_sem=n_rs.at[i], device_id=(d, t), device_id_type=MESH,
        )

    def copy_m(i, who):
        d = grp_at(g, i)
        return pltpu.make_async_remote_copy(
            src_ref=send_m.at[d], dst_ref=metav.at[who],
            send_sem=m_ss.at[i], recv_sem=m_rs.at[i], device_id=(d, t), device_id_type=MESH,
        )

    def copy_za(i, who):
        u = lax.rem(t + i, TP)
        return pltpu.make_async_remote_copy(
            src_ref=recv_a.at[:, u], dst_ref=pages.at[:, 0, :, cols(who)],
            send_sem=za_ss.at[i], recv_sem=za_rs.at[i], device_id=(g, u), device_id_type=MESH,
        )

    def copy_zb(i, who):
        u = lax.rem(t + i, TP)
        return pltpu.make_async_remote_copy(
            src_ref=zsend_b.at[:, u], dst_ref=zrecv_b.at[:, :, cols(who)],
            send_sem=zb_ss.at[i], recv_sem=zb_rs.at[i], device_id=(g, u), device_id_type=MESH,
        )

    def copy_zn(i, who):
        u = lax.rem(t + i, TP)
        return pltpu.make_async_remote_copy(
            src_ref=zsend_n.at[:, u], dst_ref=zrecv_n.at[:, :, cols(who)],
            send_sem=zn_ss.at[i], recv_sem=zn_rs.at[i], device_id=(g, u), device_id_type=MESH,
        )

    def start_grp(copy):
        for i in range(1, GRP):
            copy(i, g).start()

    def start_tp(copy):
        for i in range(1, TP):
            copy(i, t).start()

    def arrived_grp(copy):
        for i in range(1, GRP):
            copy(i, grp_back(g, i)).wait_recv()

    def arrived_tp(copy):
        for i in range(1, TP):
            copy(i, lax.rem(t + TP - i, TP)).wait_recv()

    def sent_grp(copy):
        for i in range(1, GRP):
            copy(i, g).wait_send()

    def sent_tp(copy):
        for i in range(1, TP):
            copy(i, t).wait_send()

    own_a = pltpu.make_async_copy(send_a.at[two(g)], recv_a.at[two(g)], own_sem.at[0])
    own_zb = pltpu.make_async_copy(zsend_b.at[:, t], zrecv_b.at[:, :, cols(t)], own_sem.at[1])
    own_zn = pltpu.make_async_copy(zsend_n.at[:, t], zrecv_n.at[:, :, cols(t)], own_sem.at[2])
    own_b = pltpu.make_async_copy(
        send_b.at[two(g)], pages.at[two(g), pl.ds(1, PG - 1)], own_sem.at[3]
    )
    own_n = pltpu.make_async_copy(send_n.at[two(g)], fresh.at[two(g)], own_sem.at[4])
    own_m = pltpu.make_async_copy(send_m.at[g], metav.at[g], own_sem.at[5])
    own_za = pltpu.make_async_copy(recv_a.at[:, t], pages.at[:, 0, :, cols(t)], own_sem.at[6])
    meta_copy = pltpu.make_async_copy(metav, metas, own_sem.at[7])

    start_grp(copy_a)
    start_tp(copy_zb)
    own_a.start()
    own_zb.start()

    def pack_m(d, _):
        _, _, n0 = slot_of(PAIR * d)
        _, _, n1 = slot_of(PAIR * d + 1)
        row = lax.broadcasted_iota(jnp.int32, (8, 128), 0)
        send_m[d] = jnp.where(row == 0, n0, n1)
        return 0

    lax.fori_loop(0, GRP, pack_m, 0)
    start_grp(copy_m)
    own_m.start()

    for k in range(width // HS):
        gains[:, k * HS : (k + 1) * HS] = jnp.broadcast_to(gain[k : k + 1, :], (16, HS))

    loads[1].wait()
    loads[2].wait()
    for b in range(blocks):
        loads[3 + b].wait()

    def rotated(values, n):
        return values * cos_ref[n] + pltpu.roll(values, HS // 2, 1) * sin_ref[n]

    def kv_block(b, _):
        part = pl.ds(pl.multiple_of(b * RB, RB), RB)
        ss[part, :] = jnp.zeros((RB, HS), jnp.float32)
        acc[:, 0:kvw] = jnp.zeros((RB, kvw), jnp.float32)

        def step(c, _):
            deep = pl.ds(pl.multiple_of(c * KC, KC), KC)
            x = hid[part, deep]
            xf = x.astype(jnp.float32)
            total = ss[part, :]
            for k in range(KC // HS):
                piece = xf[:, k * HS : (k + 1) * HS]
                total = total + piece * piece
            ss[part, :] = total
            xg = x * gains[0:1, deep]
            hid[part, deep] = xg
            acc[:, 0:kvw] += jnp.dot(xg, wkv[deep, :], preferred_element_type=jnp.float32)
            return 0

        lax.fori_loop(0, steps, step, 0)
        scale = lax.rsqrt(jnp.sum(ss[part, :], axis=1, keepdims=True) / width + EPS)
        ss[part, :] = jnp.broadcast_to(scale, (RB, HS))
        keys = acc[:, 0:HS] * scale + b_key[...].astype(jnp.float32)
        values = acc[:, HS:kvw] * scale + b_value[...].astype(jnp.float32)
        for r in range(per_block):
            j = b * per_block + r
            n = prefix_len[j] // PAGE
            span = slice(r * PAGE, (r + 1) * PAGE)
            joined = jnp.concatenate([rotated(keys[span], n), values[span]], axis=1)
            newkv[j] = joined.astype(jnp.bfloat16)
            zsend_n[j] = joined.reshape(TP, PAGE // TP, kvw).astype(jnp.bfloat16)
        return 0

    lax.fori_loop(0, blocks, kv_block, 0)
    start_tp(copy_zn)
    own_zn.start()

    arrived_tp(copy_zb)
    own_zb.wait()

    def pack_b(d, _):
        for k in range(PAIR):
            slot = PAIR * d + k
            used, jc, n = slot_of(slot)
            for p in range(1, PG):
                page = zrecv_b[(p - 1) * requests + jc]
                send_b[slot, p - 1] = jnp.where(n > p, page, jnp.zeros_like(page))
        return 0

    lax.fori_loop(0, GRP, pack_b, 0)
    start_grp(copy_b)
    own_b.start()

    arrived_grp(copy_a)
    own_a.wait()
    start_tp(copy_za)
    own_za.start()

    loads[3 + blocks].wait()

    def q_block(b, _):
        part = pl.ds(pl.multiple_of(b * RB, RB), RB)
        acc[...] = jnp.zeros(acc.shape, jnp.float32)

        def step(c, _):
            deep = pl.ds(pl.multiple_of(c * KC, KC), KC)
            acc[...] += jnp.dot(hid[part, deep], wq[deep, :], preferred_element_type=jnp.float32)
            return 0

        lax.fori_loop(0, steps, step, 0)
        scale = ss[part, :]
        for h in range(wq.shape[1] // HS):
            lanes = slice(h * HS, (h + 1) * HS)
            one = acc[:, lanes] * scale + b_query[h : h + 1, :].astype(jnp.float32)
            for r in range(per_block):
                j = b * per_block + r
                n = prefix_len[j] // PAGE
                turned = rotated(one[r * PAGE : (r + 1) * PAGE], n)
                qrot[j, h * PAGE : (h + 1) * PAGE, :] = turned.astype(jnp.bfloat16)
        return 0

    lax.fori_loop(0, blocks, q_block, 0)

    arrived_tp(copy_zn)
    own_zn.wait()

    def pack_n(d, _):
        for k in range(PAIR):
            slot = PAIR * d + k
            used, jc, n = slot_of(slot)
            page = zrecv_n[jc]
            send_n[slot] = jnp.where(used, page, jnp.zeros_like(page))
        return 0

    lax.fori_loop(0, GRP, pack_n, 0)
    start_grp(copy_n)
    own_n.start()

    arrived_grp(copy_m)
    own_m.wait()
    meta_copy.start()

    heads = wq.shape[1] // HS
    qrows = heads * PAGE
    length = (PG + 1) * PAGE

    def attend(j, _):
        n = prefix_len[j] // PAGE
        pages = [poolv[page_table[p, j]].reshape(PAGE, kvw) for p in range(PG)]
        pages.append(newkv[j])
        kv = jnp.concatenate(pages, axis=0)
        scores = lax.dot_general(
            qrot[j], kv[:, 0:HS], (((1,), (1,)), ((), ())), preferred_element_type=jnp.float32
        ) * (1.0 / math.sqrt(HS))
        column = lax.broadcasted_iota(jnp.int32, (qrows, length), 1)
        token = lax.rem(lax.broadcasted_iota(jnp.int32, (qrows, length), 0), PAGE)
        limit = jnp.where(column < PG * PAGE, n * PAGE, token + (PG * PAGE + 1))
        scores = jnp.where(column < limit, scores, -1e30)
        highest = jnp.max(scores, axis=1, keepdims=True)
        weights = jnp.exp(scores - highest)
        total = jnp.sum(weights, axis=1, keepdims=True)
        out = jnp.dot(weights.astype(jnp.bfloat16), kv[:, HS:kvw], preferred_element_type=jnp.float32)
        out = (out / total).astype(jnp.bfloat16)
        span = pl.ds(pl.multiple_of(j * PAGE, PAGE), PAGE)
        for h in range(heads):
            attnv[span, h * HS : (h + 1) * HS] = out[h * PAGE : (h + 1) * PAGE]
        return 0

    lax.fori_loop(0, requests, attend, 0)

    meta_copy.wait()
    arrived_tp(copy_za)
    own_za.wait()
    arrived_grp(copy_b)
    own_b.wait()

    def place(who):
        for k in range(PAIR):
            slot = PAIR * who + k
            n = metas[who, k, 0]
            page = fresh[slot]
            for p in range(PG):
                pages[slot, p] = jnp.where(n == p, page, pages[slot, p])
            pages[slot, PG] = jnp.where(n == PG, page, jnp.zeros_like(page))

    own_n.wait()
    place(g)
    for i in range(1, GRP):
        who = grp_back(g, i)
        copy_n(i, who).wait_recv()
        place(who)
    sent_tp(copy_zb)
    sent_grp(copy_a)
    sent_grp(copy_m)
    sent_tp(copy_zn)
    sent_grp(copy_b)
    sent_tp(copy_za)
    sent_grp(copy_n)


def local(
    hidden, norm_gain, w_query, b_query, w_key, b_key, w_value, b_value,
    kv_pool, page_table, prefix_len, request_group,
):
    rows, width = hidden.shape
    qw = w_query.shape[1]
    requests = prefix_len.shape[0]
    npool = kv_pool.shape[0]
    kvw = kv_pool.shape[2]
    page_rows = PAGE // TP
    full = TP * kvw
    slots = PAIR * GRP
    bf = jnp.bfloat16
    cosine, sine = rope_tables()
    any_ = pl.BlockSpec(memory_space=pl.ANY)
    vmem = pl.BlockSpec(memory_space=pltpu.VMEM)
    smem = pl.BlockSpec(memory_space=pltpu.SMEM)
    dma = pltpu.SemaphoreType.DMA
    attn, pages = pl.pallas_call(
        main_kernel,
        name="span_and_routes",
        out_shape=[
            pltpu.VMEM((rows, qw), bf),
            pltpu.VMEM((slots, PG + 1, page_rows, full), bf),
        ],
        in_specs=[any_, vmem, any_, vmem, any_, vmem, any_, vmem, any_, vmem, vmem, smem, smem, smem],
        out_specs=[vmem, vmem],
        scratch_shapes=[
            pltpu.VMEM((rows, width), bf),
            pltpu.VMEM((width, qw), bf),
            pltpu.VMEM((width, 2 * HS), bf),
            pltpu.VMEM((npool, TP, page_rows, kvw), bf),
            pltpu.VMEM((rows, HS), jnp.float32),
            pltpu.VMEM((RB, qw), jnp.float32),
            pltpu.VMEM((requests, PAGE, kvw), bf),
            pltpu.VMEM((requests, qw // HS * PAGE, HS), bf),
            pltpu.VMEM((slots, page_rows, full), bf),
            pltpu.VMEM((GRP, 8, 128), jnp.int32),
            pltpu.SMEM((GRP, 8, 128), jnp.int32),
            pltpu.VMEM((16, width), bf),
            pltpu.VMEM((slots, TP, page_rows, kvw), bf),
            pltpu.VMEM((slots, TP, page_rows, kvw), bf),
            pltpu.VMEM(((PG - 1) * requests, TP, page_rows, kvw), bf),
            pltpu.VMEM(((PG - 1) * requests, page_rows, full), bf),
            pltpu.VMEM((requests, TP, page_rows, kvw), bf),
            pltpu.VMEM((requests, page_rows, full), bf),
            pltpu.VMEM((slots, PG - 1, page_rows, full), bf),
            pltpu.VMEM((slots, page_rows, full), bf),
            pltpu.VMEM((GRP, 8, 128), jnp.int32),
            pltpu.SMEM((slots,), jnp.int32),
            dma((4 + rows // RB,)),
            dma((8,)),
            dma((GRP,)), dma((GRP,)),
            dma((GRP,)), dma((GRP,)),
            dma((GRP,)), dma((GRP,)),
            dma((GRP,)), dma((GRP,)),
            dma((TP,)), dma((TP,)),
            dma((TP,)), dma((TP,)),
            dma((TP,)), dma((TP,)),
        ],
        cost_estimate=pl.CostEstimate(
            flops=2 * rows * width * (qw + 2 * HS), bytes_accessed=40 << 20, transcendentals=0
        ),
        compiler_params=pltpu.CompilerParams(
            collective_id=0, has_side_effects=True, vmem_limit_bytes=58 << 20
        ),
    )(
        hidden,
        norm_gain.reshape(width // HS, HS),
        w_query,
        b_query.reshape(qw // HS, HS),
        w_key,
        b_key.reshape(1, HS),
        w_value,
        b_value.reshape(1, HS),
        kv_pool.reshape(npool, TP, page_rows, kvw),
        jnp.asarray(cosine),
        jnp.asarray(sine),
        page_table.T,
        prefix_len,
        request_group.reshape(-1),
    )
    return attn, pages.reshape(slots * (PG + 1), page_rows, full)


def solution(mesh):
    in_specs = (
        P("grp", None),
        P(),
        P(None, "tp"),
        P("tp"),
        P(None, "tp"),
        P("tp"),
        P(None, "tp"),
        P("tp"),
        P("grp", None, "tp"),
        P("grp", None),
        P("grp"),
        P(),
    )
    out_specs = (P("grp", "tp"), P("grp", "tp", None))
    return jax.shard_map(local, mesh=mesh, in_specs=in_specs, out_specs=out_specs, check_vma=False)
```

```python
import functools
import math

import jax
import jax.numpy as jnp
import numpy as np
from jax import lax
from jax.experimental import pallas as pl
from jax.experimental.pallas import tpu as pltpu
from jax.sharding import PartitionSpec as P

HS = 128
PAGE = 64
PAIR = 2
GX = 4
GY = 4
GRP = 16
TP = 8
PG = 3
ROPE_BASE = 1000000.0
EPS = 1e-06
MESH = pl.DeviceIdType.MESH
RB = 256
KC = 1024
EARLY = 2


def rope_tables():
    half = HS // 2
    inverse = np.float32(ROPE_BASE) ** (
        -(np.arange(half, dtype=np.float32) * np.float32(2.0)) / np.float32(HS)
    )
    positions = np.arange((PG + 1) * PAGE, dtype=np.float32)
    angles = (positions[:, None] * inverse.astype(np.float32)[None, :]).astype(np.float32)
    cosine = np.cos(angles.astype(np.float64)).astype(np.float32)
    sine = np.sin(angles.astype(np.float64)).astype(np.float32)
    shape = (PG + 1, PAGE, HS)
    return (
        np.concatenate([cosine, cosine], axis=1).reshape(shape),
        np.concatenate([-sine, sine], axis=1).reshape(shape),
    )


ORDER = (
    (2, 2), (2, 1), (1, 2), (2, 3), (3, 2), (2, 0), (0, 2), (1, 1),
    (3, 3), (1, 3), (3, 1), (0, 1), (1, 0), (0, 3), (3, 0),
)


def distance(i):
    dx, dy = ORDER[i - 1]
    odd = lax.rem(lax.axis_index("tp"), 2)
    dx = dx + (GX - 2 * dx) * odd if dx else dx
    dy = dy + (GY - 2 * dy) * odd if dy else dy
    return dx, dy


def grp_at(g, i):
    x, y = g // GY, lax.rem(g, GY)
    dx, dy = distance(i)
    return lax.rem(x + dx, GX) * GY + lax.rem(y + dy, GY)


def grp_back(g, i):
    x, y = g // GY, lax.rem(g, GY)
    dx, dy = distance(i)
    return lax.rem(x + GX - dx, GX) * GY + lax.rem(y + GY - dy, GY)


def main_kernel(
    hidden,
    gain_in,
    w_query,
    b_query_in,
    w_key,
    b_key_in,
    w_value,
    b_value_in,
    pool,
    cos_in,
    sin_in,
    page_table_in,
    prefix_len_in,
    request_group_in,
    attnv,
    pages,
    hid,
    wq,
    wkv,
    poolv,
    ss,
    acc,
    newkv,
    qrot,
    fresh,
    metav,
    metas,
    gains,
    send_a,
    recv_a,
    zsend_b,
    zrecv_b,
    zsend_n,
    zrecv_n,
    send_b,
    send_n,
    send_m,
    table,
    gain,
    b_query,
    b_key,
    b_value,
    cos_ref,
    sin_ref,
    page_table,
    prefix_len,
    request_group,
    small_sem,
    load_sem,
    own_sem,
    a_ss,
    a_rs,
    b_ss,
    b_rs,
    n_ss,
    n_rs,
    m_ss,
    m_rs,
    za_ss,
    za_rs,
    zb_ss,
    zb_rs,
    zn_ss,
    zn_rs,
):
    g = lax.axis_index("grp")
    t = lax.axis_index("tp")
    rows, width = hid.shape
    requests = rows // PAGE
    blocks = rows // RB
    steps = width // KC
    per_block = RB // PAGE
    kvw = 2 * HS

    def cols(who):
        return pl.ds(pl.multiple_of(who * kvw, kvw), kvw)

    loads = [
        pltpu.make_async_copy(pool, poolv, load_sem.at[0]),
        pltpu.make_async_copy(w_key, wkv.at[:, 0:HS], load_sem.at[1]),
        pltpu.make_async_copy(w_value, wkv.at[:, HS : 2 * HS], load_sem.at[2]),
    ]
    for b in range(blocks):
        part = pl.ds(b * RB, RB)
        loads.append(pltpu.make_async_copy(hidden.at[part], hid.at[part], load_sem.at[4 + b]))
    loads.append(pltpu.make_async_copy(w_query, wq, load_sem.at[3]))

    barrier = pltpu.get_barrier_semaphore()

    for i in range(1, GRP):
        pl.semaphore_signal(barrier, inc=1, device_id=(grp_at(g, i), t), device_id_type=MESH)
    for i in range(1, TP):
        pl.semaphore_signal(barrier, inc=1, device_id=(g, lax.rem(t + i, TP)), device_id_type=MESH)
    small = [
        pltpu.make_async_copy(source, target, small_sem.at[i])
        for i, (source, target) in enumerate(
            (
                (request_group_in, request_group),
                (prefix_len_in, prefix_len),
                (page_table_in, page_table),
                (gain_in, gain),
                (b_query_in, b_query),
                (b_key_in, b_key),
                (b_value_in, b_value),
                (cos_in, cos_ref),
                (sin_in, sin_ref),
            )
        )
    ]
    for load in small + loads:
        load.start()
    small[0].wait()

    def find(d, _):
        first = jnp.int32(requests)
        second = jnp.int32(requests)
        for j in range(requests - 1, -1, -1):
            hit = request_group[g * requests + j] == d
            second = jnp.where(hit, first, second)
            first = jnp.where(hit, jnp.int32(j), first)
        table[2 * d] = first
        table[2 * d + 1] = second
        return 0

    lax.fori_loop(0, GRP, find, 0)

    def slot_of(slot):
        j = table[slot]
        used = j < requests
        jc = jnp.minimum(j, requests - 1)
        n = jnp.where(used, prefix_len[jc] // PAGE, -1)
        return used, jc, n

    for load in (small[1], small[2], loads[0]):
        load.wait()

    def pack_a(d, _):
        for k in range(PAIR):
            slot = PAIR * d + k
            used, jc, n = slot_of(slot)
            for p in range(EARLY):
                page = poolv[page_table[p, jc]]
                send_a[p, slot] = jnp.where(n > p, page, jnp.zeros_like(page))
        return 0

    lax.fori_loop(0, GRP, pack_a, 0)

    def pack_zb(j, _):
        for p in range(EARLY, PG):
            zsend_b[(p - EARLY) * requests + j] = poolv[page_table[p, j]]
        return 0

    lax.fori_loop(0, requests, pack_zb, 0)

    pl.semaphore_wait(barrier, GRP - 1 + TP - 1)

    def two(who):
        return pl.ds(PAIR * who, PAIR)

    def copy_a(p):
        def made(i, who):
            d = grp_at(g, i)
            return pltpu.make_async_remote_copy(
                src_ref=send_a.at[p, two(d)], dst_ref=recv_a.at[p, two(who)],
                send_sem=a_ss.at[p, i], recv_sem=a_rs.at[p, i], device_id=(d, t), device_id_type=MESH,
            )

        return made

    def copy_b(i, who):
        d = grp_at(g, i)
        return pltpu.make_async_remote_copy(
            src_ref=send_b.at[two(d)], dst_ref=pages.at[two(who), pl.ds(EARLY, PG - EARLY)],
            send_sem=b_ss.at[i], recv_sem=b_rs.at[i], device_id=(d, t), device_id_type=MESH,
        )

    def copy_n(i, who):
        d = grp_at(g, i)
        return pltpu.make_async_remote_copy(
            src_ref=send_n.at[two(d)], dst_ref=fresh.at[two(who)],
            send_sem=n_ss.at[i], recv_sem=n_rs.at[i], device_id=(d, t), device_id_type=MESH,
        )

    def copy_m(i, who):
        d = grp_at(g, i)
        return pltpu.make_async_remote_copy(
            src_ref=send_m.at[d], dst_ref=metav.at[who],
            send_sem=m_ss.at[i], recv_sem=m_rs.at[i], device_id=(d, t), device_id_type=MESH,
        )

    def copy_za(p):
        def made(i, who):
            u = lax.rem(t + i, TP)
            return pltpu.make_async_remote_copy(
                src_ref=recv_a.at[p, :, u], dst_ref=pages.at[:, p, :, cols(who)],
                send_sem=za_ss.at[p, i], recv_sem=za_rs.at[p, i], device_id=(g, u), device_id_type=MESH,
            )

        return made

    def copy_zb(i, who):
        u = lax.rem(t + i, TP)
        return pltpu.make_async_remote_copy(
            src_ref=zsend_b.at[:, u], dst_ref=zrecv_b.at[:, :, cols(who)],
            send_sem=zb_ss.at[i], recv_sem=zb_rs.at[i], device_id=(g, u), device_id_type=MESH,
        )

    def copy_zn(i, who):
        u = lax.rem(t + i, TP)
        return pltpu.make_async_remote_copy(
            src_ref=zsend_n.at[:, u], dst_ref=zrecv_n.at[:, :, cols(who)],
            send_sem=zn_ss.at[i], recv_sem=zn_rs.at[i], device_id=(g, u), device_id_type=MESH,
        )

    def start_grp(copy):
        for i in range(1, GRP):
            copy(i, g).start()

    def start_tp(copy):
        for i in range(1, TP):
            copy(i, t).start()

    def arrived_grp(copy):
        for i in range(1, GRP):
            copy(i, grp_back(g, i)).wait_recv()

    def arrived_tp(copy):
        for i in range(1, TP):
            copy(i, lax.rem(t + TP - i, TP)).wait_recv()

    def sent_grp(copy):
        for i in range(1, GRP):
            copy(i, g).wait_send()

    def sent_tp(copy):
        for i in range(1, TP):
            copy(i, t).wait_send()

    own_a = pltpu.make_async_copy(send_a.at[:, two(g)], recv_a.at[:, two(g)], own_sem.at[0])
    own_zb = pltpu.make_async_copy(zsend_b.at[:, t], zrecv_b.at[:, :, cols(t)], own_sem.at[1])
    own_zn = pltpu.make_async_copy(zsend_n.at[:, t], zrecv_n.at[:, :, cols(t)], own_sem.at[2])
    own_b = pltpu.make_async_copy(
        send_b.at[two(g)], pages.at[two(g), pl.ds(EARLY, PG - EARLY)], own_sem.at[3]
    )
    own_n = pltpu.make_async_copy(send_n.at[two(g)], fresh.at[two(g)], own_sem.at[4])
    own_m = pltpu.make_async_copy(send_m.at[g], metav.at[g], own_sem.at[5])
    own_za = [
        pltpu.make_async_copy(recv_a.at[p, :, t], pages.at[:, p, :, cols(t)], own_sem.at[8 + p])
        for p in range(EARLY)
    ]
    meta_copy = pltpu.make_async_copy(metav, metas, own_sem.at[7])

    start_grp(copy_a(0))
    start_tp(copy_zb)
    for p in range(1, EARLY):
        start_grp(copy_a(p))
    own_a.start()
    own_zb.start()

    def pack_m(d, _):
        _, _, n0 = slot_of(PAIR * d)
        _, _, n1 = slot_of(PAIR * d + 1)
        row = lax.broadcasted_iota(jnp.int32, (8, 128), 0)
        send_m[d] = jnp.where(row == 0, n0, n1)
        return 0

    lax.fori_loop(0, GRP, pack_m, 0)
    start_grp(copy_m)
    own_m.start()

    for load in small[3:]:
        load.wait()
    for k in range(width // HS):
        gains[:, k * HS : (k + 1) * HS] = jnp.broadcast_to(gain[k : k + 1, :], (16, HS))

    loads[1].wait()
    loads[2].wait()
    for b in range(blocks):
        loads[3 + b].wait()

    def rotated(values, n):
        return values * cos_ref[n] + pltpu.roll(values, HS // 2, 1) * sin_ref[n]

    def kv_block(b, _):
        part = pl.ds(pl.multiple_of(b * RB, RB), RB)
        ss[part, :] = jnp.zeros((RB, HS), jnp.float32)
        acc[:, 0:kvw] = jnp.zeros((RB, kvw), jnp.float32)

        def step(c, _):
            deep = pl.ds(pl.multiple_of(c * KC, KC), KC)
            x = hid[part, deep]
            xf = x.astype(jnp.float32)
            total = ss[part, :]
            for k in range(KC // HS):
                piece = xf[:, k * HS : (k + 1) * HS]
                total = total + piece * piece
            ss[part, :] = total
            xg = x * gains[0:1, deep]
            hid[part, deep] = xg
            acc[:, 0:kvw] += jnp.dot(xg, wkv[deep, :], preferred_element_type=jnp.float32)
            return 0

        lax.fori_loop(0, steps, step, 0)
        scale = lax.rsqrt(jnp.sum(ss[part, :], axis=1, keepdims=True) / width + EPS)
        ss[part, :] = jnp.broadcast_to(scale, (RB, HS))
        keys = acc[:, 0:HS] * scale + b_key[...].astype(jnp.float32)
        values = acc[:, HS:kvw] * scale + b_value[...].astype(jnp.float32)
        for r in range(per_block):
            j = b * per_block + r
            n = prefix_len[j] // PAGE
            span = slice(r * PAGE, (r + 1) * PAGE)
            joined = jnp.concatenate([rotated(keys[span], n), values[span]], axis=1)
            newkv[j] = joined.astype(jnp.bfloat16)
            zsend_n[j] = joined.reshape(TP, PAGE // TP, kvw).astype(jnp.bfloat16)
        return 0

    lax.fori_loop(0, blocks, kv_block, 0)
    start_tp(copy_zn)
    own_zn.start()

    arrived_tp(copy_zb)
    own_zb.wait()

    def pack_b(d, _):
        for k in range(PAIR):
            slot = PAIR * d + k
            used, jc, n = slot_of(slot)
            for p in range(EARLY, PG):
                page = zrecv_b[(p - EARLY) * requests + jc]
                send_b[slot, p - EARLY] = jnp.where(n > p, page, jnp.zeros_like(page))
        return 0

    lax.fori_loop(0, GRP, pack_b, 0)
    start_grp(copy_b)
    own_b.start()

    def pass_on(p):
        arrived_grp(copy_a(p))
        if p == 0:
            own_a.wait()
        start_tp(copy_za(p))
        own_za[p].start()

    pass_on(0)

    loads[3 + blocks].wait()

    def q_block(b, _):
        part = pl.ds(pl.multiple_of(b * RB, RB), RB)
        acc[...] = jnp.zeros(acc.shape, jnp.float32)

        def step(c, _):
            deep = pl.ds(pl.multiple_of(c * KC, KC), KC)
            acc[...] += jnp.dot(hid[part, deep], wq[deep, :], preferred_element_type=jnp.float32)
            return 0

        lax.fori_loop(0, steps, step, 0)
        scale = ss[part, :]
        for h in range(wq.shape[1] // HS):
            lanes = slice(h * HS, (h + 1) * HS)
            one = acc[:, lanes] * scale + b_query[h : h + 1, :].astype(jnp.float32)
            for r in range(per_block):
                j = b * per_block + r
                n = prefix_len[j] // PAGE
                turned = rotated(one[r * PAGE : (r + 1) * PAGE], n)
                qrot[j, h * PAGE : (h + 1) * PAGE, :] = turned.astype(jnp.bfloat16)
        return 0

    lax.fori_loop(0, blocks // 2, q_block, 0)

    arrived_tp(copy_zn)
    own_zn.wait()

    def pack_n(d, _):
        for k in range(PAIR):
            slot = PAIR * d + k
            used, jc, n = slot_of(slot)
            page = zrecv_n[jc]
            send_n[slot] = jnp.where(used, page, jnp.zeros_like(page))
        return 0

    lax.fori_loop(0, GRP, pack_n, 0)
    start_grp(copy_n)
    own_n.start()

    for p in range(1, EARLY):
        pass_on(p)
    lax.fori_loop(blocks // 2, blocks, q_block, 0)

    arrived_grp(copy_m)
    own_m.wait()
    meta_copy.start()

    heads = wq.shape[1] // HS
    qrows = heads * PAGE
    length = (PG + 1) * PAGE

    def attend(j, _):
        n = prefix_len[j] // PAGE
        pages = [poolv[page_table[p, j]].reshape(PAGE, kvw) for p in range(PG)]
        pages.append(newkv[j])
        kv = jnp.concatenate(pages, axis=0)
        scores = lax.dot_general(
            qrot[j], kv[:, 0:HS], (((1,), (1,)), ((), ())), preferred_element_type=jnp.float32
        ) * (1.0 / math.sqrt(HS))
        column = lax.broadcasted_iota(jnp.int32, (qrows, length), 1)
        token = lax.rem(lax.broadcasted_iota(jnp.int32, (qrows, length), 0), PAGE)
        limit = jnp.where(column < PG * PAGE, n * PAGE, token + (PG * PAGE + 1))
        scores = jnp.where(column < limit, scores, -1e30)
        highest = jnp.max(scores, axis=1, keepdims=True)
        weights = jnp.exp(scores - highest)
        total = jnp.sum(weights, axis=1, keepdims=True)
        out = jnp.dot(weights.astype(jnp.bfloat16), kv[:, HS:kvw], preferred_element_type=jnp.float32)
        out = (out / total).astype(jnp.bfloat16)
        span = pl.ds(pl.multiple_of(j * PAGE, PAGE), PAGE)
        for h in range(heads):
            attnv[span, h * HS : (h + 1) * HS] = out[h * PAGE : (h + 1) * PAGE]
        return 0

    lax.fori_loop(0, requests, attend, 0)

    meta_copy.wait()
    for p in range(EARLY):
        arrived_tp(copy_za(p))
        own_za[p].wait()
    arrived_grp(copy_b)
    own_b.wait()

    def place(who):
        for k in range(PAIR):
            slot = PAIR * who + k
            n = metas[who, k, 0]
            page = fresh[slot]
            for p in range(PG):
                pages[slot, p] = jnp.where(n == p, page, pages[slot, p])
            pages[slot, PG] = jnp.where(n == PG, page, jnp.zeros_like(page))

    own_n.wait()
    place(g)
    for i in range(1, GRP):
        who = grp_back(g, i)
        copy_n(i, who).wait_recv()
        place(who)
    sent_tp(copy_zb)
    for p in range(EARLY):
        sent_grp(copy_a(p))
        sent_tp(copy_za(p))
    sent_grp(copy_m)
    sent_tp(copy_zn)
    sent_grp(copy_b)
    sent_grp(copy_n)


def out_kernel(attnv, pagesv, attn, pages, sems):
    rows, slots = attnv.shape[0], pagesv.shape[0]
    copies = []
    for i in range(slots // 4):
        part = pl.ds(i * 4, 4)
        copies.append(pltpu.make_async_copy(pagesv.at[part], pages.at[part], sems.at[i]))
    for i in range(2):
        part = pl.ds(i * (rows // 2), rows // 2)
        copies.append(
            pltpu.make_async_copy(attnv.at[part], attn.at[part], sems.at[slots // 4 + i])
        )
    for copy in copies:
        copy.start()
    for copy in copies:
        copy.wait()


def local(
    hidden, norm_gain, w_query, b_query, w_key, b_key, w_value, b_value,
    kv_pool, page_table, prefix_len, request_group,
):
    rows, width = hidden.shape
    qw = w_query.shape[1]
    requests = prefix_len.shape[0]
    npool = kv_pool.shape[0]
    kvw = kv_pool.shape[2]
    page_rows = PAGE // TP
    full = TP * kvw
    slots = PAIR * GRP
    bf = jnp.bfloat16
    cosine, sine = rope_tables()
    any_ = pl.BlockSpec(memory_space=pl.ANY)
    vmem = pl.BlockSpec(memory_space=pltpu.VMEM)
    dma = pltpu.SemaphoreType.DMA
    attn, pages = pl.pallas_call(
        main_kernel,
        name="span_and_routes",
        out_shape=[
            pltpu.VMEM((rows, qw), bf),
            pltpu.VMEM((slots, PG + 1, page_rows, full), bf),
        ],
        in_specs=[any_] * 14,
        out_specs=[vmem, vmem],
        scratch_shapes=[
            pltpu.VMEM((rows, width), bf),
            pltpu.VMEM((width, qw), bf),
            pltpu.VMEM((width, 2 * HS), bf),
            pltpu.VMEM((npool, TP, page_rows, kvw), bf),
            pltpu.VMEM((rows, HS), jnp.float32),
            pltpu.VMEM((RB, qw), jnp.float32),
            pltpu.VMEM((requests, PAGE, kvw), bf),
            pltpu.VMEM((requests, qw // HS * PAGE, HS), bf),
            pltpu.VMEM((slots, page_rows, full), bf),
            pltpu.VMEM((GRP, 8, 128), jnp.int32),
            pltpu.SMEM((GRP, 8, 128), jnp.int32),
            pltpu.VMEM((16, width), bf),
            pltpu.VMEM((EARLY, slots, TP, page_rows, kvw), bf),
            pltpu.VMEM((EARLY, slots, TP, page_rows, kvw), bf),
            pltpu.VMEM(((PG - EARLY) * requests, TP, page_rows, kvw), bf),
            pltpu.VMEM(((PG - EARLY) * requests, page_rows, full), bf),
            pltpu.VMEM((requests, TP, page_rows, kvw), bf),
            pltpu.VMEM((requests, page_rows, full), bf),
            pltpu.VMEM((slots, PG - EARLY, page_rows, full), bf),
            pltpu.VMEM((slots, page_rows, full), bf),
            pltpu.VMEM((GRP, 8, 128), jnp.int32),
            pltpu.SMEM((slots,), jnp.int32),
            pltpu.VMEM((width // HS, HS), bf),
            pltpu.VMEM((qw // HS, HS), bf),
            pltpu.VMEM((1, HS), bf),
            pltpu.VMEM((1, HS), bf),
            pltpu.VMEM(cosine.shape, jnp.float32),
            pltpu.VMEM(sine.shape, jnp.float32),
            pltpu.SMEM((PG, requests), jnp.int32),
            pltpu.SMEM((requests,), jnp.int32),
            pltpu.SMEM((request_group.shape[0],), jnp.int32),
            dma((9,)),
            dma((4 + rows // RB,)),
            dma((8 + EARLY,)),
            dma((EARLY, GRP)), dma((EARLY, GRP)),
            dma((GRP,)), dma((GRP,)),
            dma((GRP,)), dma((GRP,)),
            dma((GRP,)), dma((GRP,)),
            dma((EARLY, TP)), dma((EARLY, TP)),
            dma((TP,)), dma((TP,)),
            dma((TP,)), dma((TP,)),
        ],
        cost_estimate=pl.CostEstimate(
            flops=2 * rows * width * (qw + 2 * HS), bytes_accessed=40 << 20, transcendentals=0
        ),
        compiler_params=pltpu.CompilerParams(
            collective_id=0, has_side_effects=True, vmem_limit_bytes=58 << 20
        ),
    )(
        hidden,
        norm_gain.reshape(width // HS, HS),
        w_query,
        b_query.reshape(qw // HS, HS),
        w_key,
        b_key.reshape(1, HS),
        w_value,
        b_value.reshape(1, HS),
        kv_pool.reshape(npool, TP, page_rows, kvw),
        jnp.asarray(cosine),
        jnp.asarray(sine),
        page_table.T,
        prefix_len,
        request_group.reshape(-1),
    )
    attn, pages = pl.pallas_call(
        out_kernel,
        name="write_out",
        out_shape=[
            jax.ShapeDtypeStruct(attn.shape, bf),
            jax.ShapeDtypeStruct(pages.shape, bf),
        ],
        in_specs=[vmem, vmem],
        out_specs=[any_, any_],
        scratch_shapes=[dma((2 + slots // 4,))],
        compiler_params=pltpu.CompilerParams(vmem_limit_bytes=1 << 20),
    )(attn, pages)
    return attn, pages.reshape(slots * (PG + 1), page_rows, full)


def solution(mesh):
    in_specs = (
        P("grp", None),
        P(),
        P(None, "tp"),
        P("tp"),
        P(None, "tp"),
        P("tp"),
        P(None, "tp"),
        P("tp"),
        P("grp", None, "tp"),
        P("grp", None),
        P("grp"),
        P(),
    )
    out_specs = (P("grp", "tp"), P("grp", "tp", None))
    return jax.shard_map(local, mesh=mesh, in_specs=in_specs, out_specs=out_specs, check_vma=False)
```

```python
import functools
import math

import jax
import jax.numpy as jnp
import numpy as np
from jax import lax
from jax.experimental import pallas as pl
from jax.experimental.pallas import tpu as pltpu
from jax.sharding import PartitionSpec as P

HS = 128
PAGE = 64
PAIR = 2
GX = 4
GY = 4
GRP = 16
TP = 8
PG = 3
ROPE_BASE = 1000000.0
EPS = 1e-06
MESH = pl.DeviceIdType.MESH
RB = 256
KC = 1024
EARLY = 2


def rope_tables():
    half = HS // 2
    inverse = np.float32(ROPE_BASE) ** (
        -(np.arange(half, dtype=np.float32) * np.float32(2.0)) / np.float32(HS)
    )
    positions = np.arange((PG + 1) * PAGE, dtype=np.float32)
    angles = (positions[:, None] * inverse.astype(np.float32)[None, :]).astype(np.float32)
    cosine = np.cos(angles.astype(np.float64)).astype(np.float32)
    sine = np.sin(angles.astype(np.float64)).astype(np.float32)
    shape = (PG + 1, PAGE, HS)
    return (
        np.concatenate([cosine, cosine], axis=1).reshape(shape),
        np.concatenate([-sine, sine], axis=1).reshape(shape),
    )


ORDER = (
    (2, 2), (2, 1), (1, 2), (2, 3), (3, 2), (2, 0), (0, 2), (1, 1),
    (3, 3), (1, 3), (3, 1), (0, 1), (3, 0), (0, 3), (1, 0),
)


def distance(i):
    dx, dy = ORDER[i - 1]
    odd = lax.rem(lax.axis_index("tp"), 2)
    dx = dx + (GX - 2 * dx) * odd if dx else dx
    dy = dy + (GY - 2 * dy) * odd if dy else dy
    return dx, dy


def grp_at(g, i):
    x, y = g // GY, lax.rem(g, GY)
    dx, dy = distance(i)
    return lax.rem(x + dx, GX) * GY + lax.rem(y + dy, GY)


def grp_back(g, i):
    x, y = g // GY, lax.rem(g, GY)
    dx, dy = distance(i)
    return lax.rem(x + GX - dx, GX) * GY + lax.rem(y + GY - dy, GY)


def main_kernel(
    hidden,
    gain_in,
    w_query,
    b_query_in,
    w_key,
    b_key_in,
    w_value,
    b_value_in,
    pool,
    cos_in,
    sin_in,
    page_table_in,
    prefix_len_in,
    request_group_in,
    attnv,
    pages,
    hid,
    wq,
    wkv,
    poolv,
    ss,
    acc,
    newkv,
    qrot,
    fresh,
    metav,
    metas,
    gains,
    send_a,
    recv_a,
    zsend_b,
    zrecv_b,
    zsend_n,
    zrecv_n,
    send_b,
    send_n,
    send_m,
    table,
    gain,
    b_query,
    b_key,
    b_value,
    cos_ref,
    sin_ref,
    page_table,
    prefix_len,
    request_group,
    small_sem,
    load_sem,
    own_sem,
    a_ss,
    a_rs,
    b_ss,
    b_rs,
    n_ss,
    n_rs,
    m_ss,
    m_rs,
    za_ss,
    za_rs,
    zb_ss,
    zb_rs,
    zn_ss,
    zn_rs,
):
    g = lax.axis_index("grp")
    t = lax.axis_index("tp")
    rows, width = hid.shape
    requests = rows // PAGE
    blocks = rows // RB
    steps = width // KC
    per_block = RB // PAGE
    kvw = 2 * HS

    def cols(who):
        return pl.ds(pl.multiple_of(who * kvw, kvw), kvw)

    loads = [
        pltpu.make_async_copy(pool, poolv, load_sem.at[0]),
        pltpu.make_async_copy(w_key, wkv.at[:, 0:HS], load_sem.at[1]),
        pltpu.make_async_copy(w_value, wkv.at[:, HS : 2 * HS], load_sem.at[2]),
    ]
    for b in range(blocks):
        part = pl.ds(b * RB, RB)
        loads.append(pltpu.make_async_copy(hidden.at[part], hid.at[part], load_sem.at[4 + b]))
    loads.append(pltpu.make_async_copy(w_query, wq, load_sem.at[3]))

    barrier = pltpu.get_barrier_semaphore()

    for i in range(1, GRP):
        pl.semaphore_signal(barrier, inc=1, device_id=(grp_at(g, i), t), device_id_type=MESH)
    for i in range(1, TP):
        pl.semaphore_signal(barrier, inc=1, device_id=(g, lax.rem(t + i, TP)), device_id_type=MESH)
    small = [
        pltpu.make_async_copy(source, target, small_sem.at[i])
        for i, (source, target) in enumerate(
            (
                (request_group_in, request_group),
                (prefix_len_in, prefix_len),
                (page_table_in, page_table),
                (gain_in, gain),
                (b_query_in, b_query),
                (b_key_in, b_key),
                (b_value_in, b_value),
                (cos_in, cos_ref),
                (sin_in, sin_ref),
            )
        )
    ]
    for load in small + loads:
        load.start()
    small[0].wait()

    def find(d, _):
        first = jnp.int32(requests)
        second = jnp.int32(requests)
        for j in range(requests - 1, -1, -1):
            hit = request_group[g * requests + j] == d
            second = jnp.where(hit, first, second)
            first = jnp.where(hit, jnp.int32(j), first)
        table[2 * d] = first
        table[2 * d + 1] = second
        return 0

    lax.fori_loop(0, GRP, find, 0)

    def slot_of(slot):
        j = table[slot]
        used = j < requests
        jc = jnp.minimum(j, requests - 1)
        n = jnp.where(used, prefix_len[jc] // PAGE, -1)
        return used, jc, n

    for load in (small[1], small[2], loads[0]):
        load.wait()

    def pack_a(d, _):
        for k in range(PAIR):
            slot = PAIR * d + k
            used, jc, n = slot_of(slot)
            for p in range(EARLY):
                page = poolv[page_table[p, jc]]
                send_a[p, slot] = jnp.where(n > p, page, jnp.zeros_like(page))
        return 0

    lax.fori_loop(0, GRP, pack_a, 0)

    def pack_zb(j, _):
        for p in range(EARLY, PG):
            zsend_b[(p - EARLY) * requests + j] = poolv[page_table[p, j]]
        return 0

    lax.fori_loop(0, requests, pack_zb, 0)

    pl.semaphore_wait(barrier, GRP - 1 + TP - 1)

    def two(who):
        return pl.ds(PAIR * who, PAIR)

    def copy_a(p):
        def made(i, who):
            d = grp_at(g, i)
            return pltpu.make_async_remote_copy(
                src_ref=send_a.at[p, two(d)], dst_ref=recv_a.at[p, two(who)],
                send_sem=a_ss.at[p, i], recv_sem=a_rs.at[p, i], device_id=(d, t), device_id_type=MESH,
            )

        return made

    def copy_b(i, who):
        d = grp_at(g, i)
        return pltpu.make_async_remote_copy(
            src_ref=send_b.at[two(d)], dst_ref=pages.at[two(who), pl.ds(EARLY, PG - EARLY)],
            send_sem=b_ss.at[i], recv_sem=b_rs.at[i], device_id=(d, t), device_id_type=MESH,
        )

    def copy_n(i, who):
        d = grp_at(g, i)
        return pltpu.make_async_remote_copy(
            src_ref=send_n.at[two(d)], dst_ref=fresh.at[two(who)],
            send_sem=n_ss.at[i], recv_sem=n_rs.at[i], device_id=(d, t), device_id_type=MESH,
        )

    def copy_m(i, who):
        d = grp_at(g, i)
        return pltpu.make_async_remote_copy(
            src_ref=send_m.at[d], dst_ref=metav.at[who],
            send_sem=m_ss.at[i], recv_sem=m_rs.at[i], device_id=(d, t), device_id_type=MESH,
        )

    def copy_za(p):
        def made(i, who):
            u = lax.rem(t + i, TP)
            return pltpu.make_async_remote_copy(
                src_ref=recv_a.at[p, :, u], dst_ref=pages.at[:, p, :, cols(who)],
                send_sem=za_ss.at[p, i], recv_sem=za_rs.at[p, i], device_id=(g, u), device_id_type=MESH,
            )

        return made

    def copy_zb(i, who):
        u = lax.rem(t + i, TP)
        return pltpu.make_async_remote_copy(
            src_ref=zsend_b.at[:, u], dst_ref=zrecv_b.at[:, :, cols(who)],
            send_sem=zb_ss.at[i], recv_sem=zb_rs.at[i], device_id=(g, u), device_id_type=MESH,
        )

    def copy_zn(i, who):
        u = lax.rem(t + i, TP)
        return pltpu.make_async_remote_copy(
            src_ref=zsend_n.at[:, u], dst_ref=zrecv_n.at[:, :, cols(who)],
            send_sem=zn_ss.at[i], recv_sem=zn_rs.at[i], device_id=(g, u), device_id_type=MESH,
        )

    def start_grp(copy):
        for i in range(1, GRP):
            copy(i, g).start()

    def start_tp(copy):
        for i in range(1, TP):
            copy(i, t).start()

    def arrived_grp(copy):
        for i in range(1, GRP):
            copy(i, grp_back(g, i)).wait_recv()

    def arrived_tp(copy):
        for i in range(1, TP):
            copy(i, lax.rem(t + TP - i, TP)).wait_recv()

    def sent_grp(copy):
        for i in range(1, GRP):
            copy(i, g).wait_send()

    def sent_tp(copy):
        for i in range(1, TP):
            copy(i, t).wait_send()

    own_a = pltpu.make_async_copy(send_a.at[:, two(g)], recv_a.at[:, two(g)], own_sem.at[0])
    own_zb = pltpu.make_async_copy(zsend_b.at[:, t], zrecv_b.at[:, :, cols(t)], own_sem.at[1])
    own_zn = pltpu.make_async_copy(zsend_n.at[:, t], zrecv_n.at[:, :, cols(t)], own_sem.at[2])
    own_b = pltpu.make_async_copy(
        send_b.at[two(g)], pages.at[two(g), pl.ds(EARLY, PG - EARLY)], own_sem.at[3]
    )
    own_n = pltpu.make_async_copy(send_n.at[two(g)], fresh.at[two(g)], own_sem.at[4])
    own_m = pltpu.make_async_copy(send_m.at[g], metav.at[g], own_sem.at[5])
    own_za = [
        pltpu.make_async_copy(recv_a.at[p, :, t], pages.at[:, p, :, cols(t)], own_sem.at[8 + p])
        for p in range(EARLY)
    ]
    meta_copy = pltpu.make_async_copy(metav, metas, own_sem.at[7])

    start_grp(copy_a(0))
    start_tp(copy_zb)
    for p in range(1, EARLY):
        start_grp(copy_a(p))
    own_a.start()
    own_zb.start()

    def pack_m(d, _):
        _, _, n0 = slot_of(PAIR * d)
        _, _, n1 = slot_of(PAIR * d + 1)
        row = lax.broadcasted_iota(jnp.int32, (8, 128), 0)
        send_m[d] = jnp.where(row == 0, n0, n1)
        return 0

    lax.fori_loop(0, GRP, pack_m, 0)
    start_grp(copy_m)
    own_m.start()

    for load in small[3:]:
        load.wait()
    for k in range(width // HS):
        gains[:, k * HS : (k + 1) * HS] = jnp.broadcast_to(gain[k : k + 1, :], (16, HS))

    loads[1].wait()
    loads[2].wait()
    for b in range(blocks):
        loads[3 + b].wait()

    def rotated(values, n):
        return values * cos_ref[n] + pltpu.roll(values, HS // 2, 1) * sin_ref[n]

    def kv_block(b, _):
        part = pl.ds(pl.multiple_of(b * RB, RB), RB)
        ss[part, :] = jnp.zeros((RB, HS), jnp.float32)
        acc[:, 0:kvw] = jnp.zeros((RB, kvw), jnp.float32)

        def step(c, _):
            deep = pl.ds(pl.multiple_of(c * KC, KC), KC)
            x = hid[part, deep]
            xf = x.astype(jnp.float32)
            total = ss[part, :]
            for k in range(KC // HS):
                piece = xf[:, k * HS : (k + 1) * HS]
                total = total + piece * piece
            ss[part, :] = total
            xg = x * gains[0:1, deep]
            hid[part, deep] = xg
            acc[:, 0:kvw] += jnp.dot(xg, wkv[deep, :], preferred_element_type=jnp.float32)
            return 0

        lax.fori_loop(0, steps, step, 0)
        scale = lax.rsqrt(jnp.sum(ss[part, :], axis=1, keepdims=True) / width + EPS)
        ss[part, :] = jnp.broadcast_to(scale, (RB, HS))
        keys = acc[:, 0:HS] * scale + b_key[...].astype(jnp.float32)
        values = acc[:, HS:kvw] * scale + b_value[...].astype(jnp.float32)
        for r in range(per_block):
            j = b * per_block + r
            n = prefix_len[j] // PAGE
            span = slice(r * PAGE, (r + 1) * PAGE)
            joined = jnp.concatenate([rotated(keys[span], n), values[span]], axis=1)
            newkv[j] = joined.astype(jnp.bfloat16)
            zsend_n[j] = joined.reshape(TP, PAGE // TP, kvw).astype(jnp.bfloat16)
        return 0

    lax.fori_loop(0, blocks, kv_block, 0)
    start_tp(copy_zn)
    own_zn.start()

    arrived_tp(copy_zb)
    own_zb.wait()

    def pack_b(d, _):
        for k in range(PAIR):
            slot = PAIR * d + k
            used, jc, n = slot_of(slot)
            for p in range(EARLY, PG):
                page = zrecv_b[(p - EARLY) * requests + jc]
                send_b[slot, p - EARLY] = jnp.where(n > p, page, jnp.zeros_like(page))
        return 0

    lax.fori_loop(0, GRP, pack_b, 0)
    start_grp(copy_b)
    own_b.start()

    def pass_on(p):
        arrived_grp(copy_a(p))
        if p == 0:
            own_a.wait()
        start_tp(copy_za(p))
        own_za[p].start()

    pass_on(0)

    loads[3 + blocks].wait()

    def q_block(b, _):
        part = pl.ds(pl.multiple_of(b * RB, RB), RB)
        acc[...] = jnp.zeros(acc.shape, jnp.float32)

        def step(c, _):
            deep = pl.ds(pl.multiple_of(c * KC, KC), KC)
            acc[...] += jnp.dot(hid[part, deep], wq[deep, :], preferred_element_type=jnp.float32)
            return 0

        lax.fori_loop(0, steps, step, 0)
        scale = ss[part, :]
        for h in range(wq.shape[1] // HS):
            lanes = slice(h * HS, (h + 1) * HS)
            one = acc[:, lanes] * scale + b_query[h : h + 1, :].astype(jnp.float32)
            for r in range(per_block):
                j = b * per_block + r
                n = prefix_len[j] // PAGE
                turned = rotated(one[r * PAGE : (r + 1) * PAGE], n)
                qrot[j, h * PAGE : (h + 1) * PAGE, :] = turned.astype(jnp.bfloat16)
        return 0

    lax.fori_loop(0, blocks // 2, q_block, 0)

    arrived_tp(copy_zn)
    own_zn.wait()

    def pack_n(d, _):
        for k in range(PAIR):
            slot = PAIR * d + k
            used, jc, n = slot_of(slot)
            page = zrecv_n[jc]
            send_n[slot] = jnp.where(used, page, jnp.zeros_like(page))
        return 0

    lax.fori_loop(0, GRP, pack_n, 0)
    start_grp(copy_n)
    own_n.start()

    for p in range(1, EARLY):
        pass_on(p)
    lax.fori_loop(blocks // 2, blocks, q_block, 0)

    arrived_grp(copy_m)
    own_m.wait()
    meta_copy.start()

    heads = wq.shape[1] // HS
    qrows = heads * PAGE
    length = (PG + 1) * PAGE

    def attend(j, _):
        n = prefix_len[j] // PAGE
        pages = [poolv[page_table[p, j]].reshape(PAGE, kvw) for p in range(PG)]
        pages.append(newkv[j])
        kv = jnp.concatenate(pages, axis=0)
        scores = lax.dot_general(
            qrot[j], kv[:, 0:HS], (((1,), (1,)), ((), ())), preferred_element_type=jnp.float32
        ) * (1.0 / math.sqrt(HS))
        column = lax.broadcasted_iota(jnp.int32, (qrows, length), 1)
        token = lax.rem(lax.broadcasted_iota(jnp.int32, (qrows, length), 0), PAGE)
        limit = jnp.where(column < PG * PAGE, n * PAGE, token + (PG * PAGE + 1))
        scores = jnp.where(column < limit, scores, -1e30)
        highest = jnp.max(scores, axis=1, keepdims=True)
        weights = jnp.exp(scores - highest)
        total = jnp.sum(weights, axis=1, keepdims=True)
        out = jnp.dot(weights.astype(jnp.bfloat16), kv[:, HS:kvw], preferred_element_type=jnp.float32)
        out = (out / total).astype(jnp.bfloat16)
        span = pl.ds(pl.multiple_of(j * PAGE, PAGE), PAGE)
        for h in range(heads):
            attnv[span, h * HS : (h + 1) * HS] = out[h * PAGE : (h + 1) * PAGE]
        return 0

    lax.fori_loop(0, requests, attend, 0)

    meta_copy.wait()
    for p in range(EARLY):
        arrived_tp(copy_za(p))
        own_za[p].wait()
    arrived_grp(copy_b)
    own_b.wait()

    def place(who):
        for k in range(PAIR):
            slot = PAIR * who + k
            n = metas[who, k, 0]
            page = fresh[slot]
            for p in range(PG):
                pages[slot, p] = jnp.where(n == p, page, pages[slot, p])
            pages[slot, PG] = jnp.where(n == PG, page, jnp.zeros_like(page))

    sent_tp(copy_zb)
    for p in range(EARLY):
        sent_grp(copy_a(p))
        sent_tp(copy_za(p))
    sent_grp(copy_m)
    sent_tp(copy_zn)
    sent_grp(copy_b)
    own_n.wait()
    place(g)
    for i in range(1, GRP):
        who = grp_back(g, i)
        copy_n(i, who).wait_recv()
        place(who)
    sent_grp(copy_n)


def out_kernel(attnv, pagesv, attn, pages, sems):
    rows, slots = attnv.shape[0], pagesv.shape[0]
    copies = []
    for i in range(slots // 4):
        part = pl.ds(i * 4, 4)
        copies.append(pltpu.make_async_copy(pagesv.at[part], pages.at[part], sems.at[i]))
    for i in range(2):
        part = pl.ds(i * (rows // 2), rows // 2)
        copies.append(
            pltpu.make_async_copy(attnv.at[part], attn.at[part], sems.at[slots // 4 + i])
        )
    for copy in copies:
        copy.start()
    for copy in copies:
        copy.wait()


def local(
    hidden, norm_gain, w_query, b_query, w_key, b_key, w_value, b_value,
    kv_pool, page_table, prefix_len, request_group,
):
    rows, width = hidden.shape
    qw = w_query.shape[1]
    requests = prefix_len.shape[0]
    npool = kv_pool.shape[0]
    kvw = kv_pool.shape[2]
    page_rows = PAGE // TP
    full = TP * kvw
    slots = PAIR * GRP
    bf = jnp.bfloat16
    cosine, sine = rope_tables()
    any_ = pl.BlockSpec(memory_space=pl.ANY)
    vmem = pl.BlockSpec(memory_space=pltpu.VMEM)
    dma = pltpu.SemaphoreType.DMA
    attn, pages = pl.pallas_call(
        main_kernel,
        name="span_and_routes",
        out_shape=[
            pltpu.VMEM((rows, qw), bf),
            pltpu.VMEM((slots, PG + 1, page_rows, full), bf),
        ],
        in_specs=[any_] * 14,
        out_specs=[vmem, vmem],
        scratch_shapes=[
            pltpu.VMEM((rows, width), bf),
            pltpu.VMEM((width, qw), bf),
            pltpu.VMEM((width, 2 * HS), bf),
            pltpu.VMEM((npool, TP, page_rows, kvw), bf),
            pltpu.VMEM((rows, HS), jnp.float32),
            pltpu.VMEM((RB, qw), jnp.float32),
            pltpu.VMEM((requests, PAGE, kvw), bf),
            pltpu.VMEM((requests, qw // HS * PAGE, HS), bf),
            pltpu.VMEM((slots, page_rows, full), bf),
            pltpu.VMEM((GRP, 8, 128), jnp.int32),
            pltpu.SMEM((GRP, 8, 128), jnp.int32),
            pltpu.VMEM((16, width), bf),
            pltpu.VMEM((EARLY, slots, TP, page_rows, kvw), bf),
            pltpu.VMEM((EARLY, slots, TP, page_rows, kvw), bf),
            pltpu.VMEM(((PG - EARLY) * requests, TP, page_rows, kvw), bf),
            pltpu.VMEM(((PG - EARLY) * requests, page_rows, full), bf),
            pltpu.VMEM((requests, TP, page_rows, kvw), bf),
            pltpu.VMEM((requests, page_rows, full), bf),
            pltpu.VMEM((slots, PG - EARLY, page_rows, full), bf),
            pltpu.VMEM((slots, page_rows, full), bf),
            pltpu.VMEM((GRP, 8, 128), jnp.int32),
            pltpu.SMEM((slots,), jnp.int32),
            pltpu.VMEM((width // HS, HS), bf),
            pltpu.VMEM((qw // HS, HS), bf),
            pltpu.VMEM((1, HS), bf),
            pltpu.VMEM((1, HS), bf),
            pltpu.VMEM(cosine.shape, jnp.float32),
            pltpu.VMEM(sine.shape, jnp.float32),
            pltpu.SMEM((PG, requests), jnp.int32),
            pltpu.SMEM((requests,), jnp.int32),
            pltpu.SMEM((request_group.shape[0],), jnp.int32),
            dma((9,)),
            dma((4 + rows // RB,)),
            dma((8 + EARLY,)),
            dma((EARLY, GRP)), dma((EARLY, GRP)),
            dma((GRP,)), dma((GRP,)),
            dma((GRP,)), dma((GRP,)),
            dma((GRP,)), dma((GRP,)),
            dma((EARLY, TP)), dma((EARLY, TP)),
            dma((TP,)), dma((TP,)),
            dma((TP,)), dma((TP,)),
        ],
        cost_estimate=pl.CostEstimate(
            flops=2 * rows * width * (qw + 2 * HS), bytes_accessed=40 << 20, transcendentals=0
        ),
        compiler_params=pltpu.CompilerParams(
            collective_id=0, has_side_effects=True, vmem_limit_bytes=58 << 20
        ),
    )(
        hidden,
        norm_gain.reshape(width // HS, HS),
        w_query,
        b_query.reshape(qw // HS, HS),
        w_key,
        b_key.reshape(1, HS),
        w_value,
        b_value.reshape(1, HS),
        kv_pool.reshape(npool, TP, page_rows, kvw),
        jnp.asarray(cosine),
        jnp.asarray(sine),
        page_table.T,
        prefix_len,
        request_group.reshape(-1),
    )
    attn, pages = pl.pallas_call(
        out_kernel,
        name="write_out",
        out_shape=[
            jax.ShapeDtypeStruct(attn.shape, bf),
            jax.ShapeDtypeStruct(pages.shape, bf),
        ],
        in_specs=[vmem, vmem],
        out_specs=[any_, any_],
        scratch_shapes=[dma((2 + slots // 4,))],
        compiler_params=pltpu.CompilerParams(vmem_limit_bytes=1 << 20),
    )(attn, pages)
    return attn, pages.reshape(slots * (PG + 1), page_rows, full)


def solution(mesh):
    in_specs = (
        P("grp", None),
        P(),
        P(None, "tp"),
        P("tp"),
        P(None, "tp"),
        P("tp"),
        P(None, "tp"),
        P("tp"),
        P("grp", None, "tp"),
        P("grp", None),
        P("grp"),
        P(),
    )
    out_specs = (P("grp", "tp"), P("grp", "tp", None))
    return jax.shard_map(local, mesh=mesh, in_specs=in_specs, out_specs=out_specs, check_vma=False)
```

```python
import functools
import math

import jax
import jax.numpy as jnp
import numpy as np
from jax import lax
from jax.experimental import pallas as pl
from jax.experimental.pallas import tpu as pltpu
from jax.sharding import PartitionSpec as P

HS = 128
PAGE = 64
PAIR = 2
GX = 4
GY = 4
GRP = 16
TP = 8
PG = 3
ROPE_BASE = 1000000.0
EPS = 1e-06
MESH = pl.DeviceIdType.MESH
RB = 256
KC = 1024
EARLY = 2


def rope_tables():
    half = HS // 2
    inverse = np.float32(ROPE_BASE) ** (
        -(np.arange(half, dtype=np.float32) * np.float32(2.0)) / np.float32(HS)
    )
    positions = np.arange((PG + 1) * PAGE, dtype=np.float32)
    angles = (positions[:, None] * inverse.astype(np.float32)[None, :]).astype(np.float32)
    cosine = np.cos(angles.astype(np.float64)).astype(np.float32)
    sine = np.sin(angles.astype(np.float64)).astype(np.float32)
    shape = (PG + 1, PAGE, HS)
    return (
        np.concatenate([cosine, cosine], axis=1).reshape(shape),
        np.concatenate([-sine, sine], axis=1).reshape(shape),
    )


ORDER = (
    (2, 2), (2, 1), (1, 2), (2, 3), (3, 2), (2, 0), (0, 2), (1, 1),
    (3, 3), (1, 3), (3, 1), (0, 1), (3, 0), (0, 3), (1, 0),
)


def distance(i):
    dx, dy = ORDER[i - 1]
    odd = lax.rem(lax.axis_index("tp"), 2)
    dx = dx + (GX - 2 * dx) * odd if dx else dx
    dy = dy + (GY - 2 * dy) * odd if dy else dy
    return dx, dy


def grp_at(g, i):
    x, y = g // GY, lax.rem(g, GY)
    dx, dy = distance(i)
    return lax.rem(x + dx, GX) * GY + lax.rem(y + dy, GY)


def grp_back(g, i):
    x, y = g // GY, lax.rem(g, GY)
    dx, dy = distance(i)
    return lax.rem(x + GX - dx, GX) * GY + lax.rem(y + GY - dy, GY)


def main_kernel(
    hidden,
    gain_in,
    w_query,
    b_query_in,
    w_key,
    b_key_in,
    w_value,
    b_value_in,
    pool,
    cos_in,
    sin_in,
    page_table_in,
    prefix_len_in,
    request_group_in,
    attnv,
    pages,
    hid,
    wq,
    wkv,
    poolv,
    ss,
    acc,
    newkv,
    qrot,
    fresh,
    metav,
    metas,
    gains,
    send_a,
    recv_a,
    zsend_b,
    zrecv_b,
    zsend_n,
    zrecv_n,
    send_b,
    send_n,
    send_m,
    table,
    gain,
    b_query,
    b_key,
    b_value,
    cos_ref,
    sin_ref,
    page_table,
    prefix_len,
    request_group,
    small_sem,
    load_sem,
    own_sem,
    a_ss,
    a_rs,
    b_ss,
    b_rs,
    n_ss,
    n_rs,
    m_ss,
    m_rs,
    za_ss,
    za_rs,
    zb_ss,
    zb_rs,
    zn_ss,
    zn_rs,
):
    g = lax.axis_index("grp")
    t = lax.axis_index("tp")
    rows, width = hid.shape
    requests = rows // PAGE
    blocks = rows // RB
    steps = width // KC
    per_block = RB // PAGE
    kvw = 2 * HS

    def cols(who):
        return pl.ds(pl.multiple_of(who * kvw, kvw), kvw)

    loads = [
        pltpu.make_async_copy(pool, poolv, load_sem.at[0]),
        pltpu.make_async_copy(w_key, wkv.at[:, 0:HS], load_sem.at[1]),
        pltpu.make_async_copy(w_value, wkv.at[:, HS : 2 * HS], load_sem.at[2]),
    ]
    for b in range(blocks):
        part = pl.ds(b * RB, RB)
        loads.append(pltpu.make_async_copy(hidden.at[part], hid.at[part], load_sem.at[4 + b]))
    loads.append(pltpu.make_async_copy(w_query, wq, load_sem.at[3]))

    barrier = pltpu.get_barrier_semaphore()

    for i in range(1, GRP):
        pl.semaphore_signal(barrier, inc=1, device_id=(grp_at(g, i), t), device_id_type=MESH)
    for i in range(1, TP):
        pl.semaphore_signal(barrier, inc=1, device_id=(g, lax.rem(t + i, TP)), device_id_type=MESH)
    small = [
        pltpu.make_async_copy(source, target, small_sem.at[i])
        for i, (source, target) in enumerate(
            (
                (request_group_in, request_group),
                (prefix_len_in, prefix_len),
                (page_table_in, page_table),
                (gain_in, gain),
                (b_query_in, b_query),
                (b_key_in, b_key),
                (b_value_in, b_value),
                (cos_in, cos_ref),
                (sin_in, sin_ref),
            )
        )
    ]
    for load in small + loads:
        load.start()
    small[0].wait()

    def find(d, _):
        first = jnp.int32(requests)
        second = jnp.int32(requests)
        for j in range(requests - 1, -1, -1):
            hit = request_group[g * requests + j] == d
            second = jnp.where(hit, first, second)
            first = jnp.where(hit, jnp.int32(j), first)
        table[2 * d] = first
        table[2 * d + 1] = second
        return 0

    lax.fori_loop(0, GRP, find, 0)

    def slot_of(slot):
        j = table[slot]
        used = j < requests
        jc = jnp.minimum(j, requests - 1)
        n = jnp.where(used, prefix_len[jc] // PAGE, -1)
        return used, jc, n

    for load in (small[1], small[2], loads[0]):
        load.wait()

    def pack_a(d, _):
        for k in range(PAIR):
            slot = PAIR * d + k
            used, jc, n = slot_of(slot)
            for p in range(EARLY):
                page = poolv[page_table[p, jc]]
                send_a[p, slot] = jnp.where(n > p, page, jnp.zeros_like(page))
        return 0

    lax.fori_loop(0, GRP, pack_a, 0)

    def pack_zb(j, _):
        for p in range(EARLY, PG):
            zsend_b[(p - EARLY) * requests + j] = poolv[page_table[p, j]]
        return 0

    lax.fori_loop(0, requests, pack_zb, 0)

    pl.semaphore_wait(barrier, GRP - 1 + TP - 1)

    def two(who):
        return pl.ds(PAIR * who, PAIR)

    def copy_a(p):
        def made(i, who):
            d = grp_at(g, i)
            return pltpu.make_async_remote_copy(
                src_ref=send_a.at[p, two(d)], dst_ref=recv_a.at[p, two(who)],
                send_sem=a_ss.at[p, i], recv_sem=a_rs.at[p, i], device_id=(d, t), device_id_type=MESH,
            )

        return made

    def copy_b(i, who):
        d = grp_at(g, i)
        return pltpu.make_async_remote_copy(
            src_ref=send_b.at[two(d)], dst_ref=pages.at[two(who), pl.ds(EARLY, PG - EARLY)],
            send_sem=b_ss.at[i], recv_sem=b_rs.at[i], device_id=(d, t), device_id_type=MESH,
        )

    def copy_n(i, who):
        d = grp_at(g, i)
        return pltpu.make_async_remote_copy(
            src_ref=send_n.at[two(d)], dst_ref=fresh.at[two(who)],
            send_sem=n_ss.at[i], recv_sem=n_rs.at[i], device_id=(d, t), device_id_type=MESH,
        )

    def copy_m(i, who):
        d = grp_at(g, i)
        return pltpu.make_async_remote_copy(
            src_ref=send_m.at[d], dst_ref=metav.at[who],
            send_sem=m_ss.at[i], recv_sem=m_rs.at[i], device_id=(d, t), device_id_type=MESH,
        )

    def copy_za(p):
        def made(i, who):
            u = lax.rem(t + i, TP)
            return pltpu.make_async_remote_copy(
                src_ref=recv_a.at[p, :, u], dst_ref=pages.at[:, p, :, cols(who)],
                send_sem=za_ss.at[p, i], recv_sem=za_rs.at[p, i], device_id=(g, u), device_id_type=MESH,
            )

        return made

    def copy_zb(i, who):
        u = lax.rem(t + i, TP)
        return pltpu.make_async_remote_copy(
            src_ref=zsend_b.at[:, u], dst_ref=zrecv_b.at[:, :, cols(who)],
            send_sem=zb_ss.at[i], recv_sem=zb_rs.at[i], device_id=(g, u), device_id_type=MESH,
        )

    def copy_zn(i, who):
        u = lax.rem(t + i, TP)
        return pltpu.make_async_remote_copy(
            src_ref=zsend_n.at[:, u], dst_ref=zrecv_n.at[:, :, cols(who)],
            send_sem=zn_ss.at[i], recv_sem=zn_rs.at[i], device_id=(g, u), device_id_type=MESH,
        )

    def start_grp(copy):
        for i in range(1, GRP):
            copy(i, g).start()

    def start_from(copy, first):
        for i in range(first, GRP):
            copy(i, g).start()
        for i in range(1, first):
            copy(i, g).start()

    def start_tp(copy):
        for i in range(1, TP):
            copy(i, t).start()

    def arrived_grp(copy):
        for i in range(1, GRP):
            copy(i, grp_back(g, i)).wait_recv()

    def arrived_tp(copy):
        for i in range(1, TP):
            copy(i, lax.rem(t + TP - i, TP)).wait_recv()

    def sent_grp(copy):
        for i in range(1, GRP):
            copy(i, g).wait_send()

    def sent_tp(copy):
        for i in range(1, TP):
            copy(i, t).wait_send()

    own_a = pltpu.make_async_copy(send_a.at[:, two(g)], recv_a.at[:, two(g)], own_sem.at[0])
    own_zb = pltpu.make_async_copy(zsend_b.at[:, t], zrecv_b.at[:, :, cols(t)], own_sem.at[1])
    own_zn = pltpu.make_async_copy(zsend_n.at[:, t], zrecv_n.at[:, :, cols(t)], own_sem.at[2])
    own_b = pltpu.make_async_copy(
        send_b.at[two(g)], pages.at[two(g), pl.ds(EARLY, PG - EARLY)], own_sem.at[3]
    )
    own_n = pltpu.make_async_copy(send_n.at[two(g)], fresh.at[two(g)], own_sem.at[4])
    own_m = pltpu.make_async_copy(send_m.at[g], metav.at[g], own_sem.at[5])
    own_za = [
        pltpu.make_async_copy(recv_a.at[p, :, t], pages.at[:, p, :, cols(t)], own_sem.at[8 + p])
        for p in range(EARLY)
    ]
    meta_copy = pltpu.make_async_copy(metav, metas, own_sem.at[7])

    start_grp(copy_a(0))
    start_tp(copy_zb)
    for p in range(1, EARLY):
        start_from(copy_a(p), 8)
    own_a.start()
    own_zb.start()

    def pack_m(d, _):
        _, _, n0 = slot_of(PAIR * d)
        _, _, n1 = slot_of(PAIR * d + 1)
        row = lax.broadcasted_iota(jnp.int32, (8, 128), 0)
        send_m[d] = jnp.where(row == 0, n0, n1)
        return 0

    lax.fori_loop(0, GRP, pack_m, 0)
    start_grp(copy_m)
    own_m.start()

    for load in small[3:]:
        load.wait()
    for k in range(width // HS):
        gains[:, k * HS : (k + 1) * HS] = jnp.broadcast_to(gain[k : k + 1, :], (16, HS))

    loads[1].wait()
    loads[2].wait()
    for b in range(blocks):
        loads[3 + b].wait()

    def rotated(values, n):
        return values * cos_ref[n] + pltpu.roll(values, HS // 2, 1) * sin_ref[n]

    def kv_block(b, _):
        part = pl.ds(pl.multiple_of(b * RB, RB), RB)
        ss[part, :] = jnp.zeros((RB, HS), jnp.float32)
        acc[:, 0:kvw] = jnp.zeros((RB, kvw), jnp.float32)

        def step(c, _):
            deep = pl.ds(pl.multiple_of(c * KC, KC), KC)
            x = hid[part, deep]
            xf = x.astype(jnp.float32)
            total = ss[part, :]
            for k in range(KC // HS):
                piece = xf[:, k * HS : (k + 1) * HS]
                total = total + piece * piece
            ss[part, :] = total
            xg = x * gains[0:1, deep]
            hid[part, deep] = xg
            acc[:, 0:kvw] += jnp.dot(xg, wkv[deep, :], preferred_element_type=jnp.float32)
            return 0

        lax.fori_loop(0, steps, step, 0)
        scale = lax.rsqrt(jnp.sum(ss[part, :], axis=1, keepdims=True) / width + EPS)
        ss[part, :] = jnp.broadcast_to(scale, (RB, HS))
        keys = acc[:, 0:HS] * scale + b_key[...].astype(jnp.float32)
        values = acc[:, HS:kvw] * scale + b_value[...].astype(jnp.float32)
        for r in range(per_block):
            j = b * per_block + r
            n = prefix_len[j] // PAGE
            span = slice(r * PAGE, (r + 1) * PAGE)
            joined = jnp.concatenate([rotated(keys[span], n), values[span]], axis=1)
            newkv[j] = joined.astype(jnp.bfloat16)
            zsend_n[j] = joined.reshape(TP, PAGE // TP, kvw).astype(jnp.bfloat16)
        return 0

    lax.fori_loop(0, blocks, kv_block, 0)
    start_tp(copy_zn)
    own_zn.start()

    arrived_tp(copy_zb)
    own_zb.wait()

    def pack_b(d, _):
        for k in range(PAIR):
            slot = PAIR * d + k
            used, jc, n = slot_of(slot)
            for p in range(EARLY, PG):
                page = zrecv_b[(p - EARLY) * requests + jc]
                send_b[slot, p - EARLY] = jnp.where(n > p, page, jnp.zeros_like(page))
        return 0

    lax.fori_loop(0, GRP, pack_b, 0)
    start_grp(copy_b)
    own_b.start()

    def pass_on(p):
        arrived_grp(copy_a(p))
        if p == 0:
            own_a.wait()
        start_tp(copy_za(p))
        own_za[p].start()

    pass_on(0)

    loads[3 + blocks].wait()

    def q_block(b, _):
        part = pl.ds(pl.multiple_of(b * RB, RB), RB)
        acc[...] = jnp.zeros(acc.shape, jnp.float32)

        def step(c, _):
            deep = pl.ds(pl.multiple_of(c * KC, KC), KC)
            acc[...] += jnp.dot(hid[part, deep], wq[deep, :], preferred_element_type=jnp.float32)
            return 0

        lax.fori_loop(0, steps, step, 0)
        scale = ss[part, :]
        for h in range(wq.shape[1] // HS):
            lanes = slice(h * HS, (h + 1) * HS)
            one = acc[:, lanes] * scale + b_query[h : h + 1, :].astype(jnp.float32)
            for r in range(per_block):
                j = b * per_block + r
                n = prefix_len[j] // PAGE
                turned = rotated(one[r * PAGE : (r + 1) * PAGE], n)
                qrot[j, h * PAGE : (h + 1) * PAGE, :] = turned.astype(jnp.bfloat16)
        return 0

    lax.fori_loop(0, blocks // 2, q_block, 0)

    arrived_tp(copy_zn)
    own_zn.wait()

    def pack_n(d, _):
        for k in range(PAIR):
            slot = PAIR * d + k
            used, jc, n = slot_of(slot)
            page = zrecv_n[jc]
            send_n[slot] = jnp.where(used, page, jnp.zeros_like(page))
        return 0

    lax.fori_loop(0, GRP, pack_n, 0)
    start_grp(copy_n)
    own_n.start()

    for p in range(1, EARLY):
        pass_on(p)
    lax.fori_loop(blocks // 2, blocks, q_block, 0)

    arrived_grp(copy_m)
    own_m.wait()
    meta_copy.start()

    heads = wq.shape[1] // HS
    qrows = heads * PAGE
    length = (PG + 1) * PAGE

    def attend(j, _):
        n = prefix_len[j] // PAGE
        pages = [poolv[page_table[p, j]].reshape(PAGE, kvw) for p in range(PG)]
        pages.append(newkv[j])
        kv = jnp.concatenate(pages, axis=0)
        scores = lax.dot_general(
            qrot[j], kv[:, 0:HS], (((1,), (1,)), ((), ())), preferred_element_type=jnp.float32
        ) * (1.0 / math.sqrt(HS))
        column = lax.broadcasted_iota(jnp.int32, (qrows, length), 1)
        token = lax.rem(lax.broadcasted_iota(jnp.int32, (qrows, length), 0), PAGE)
        limit = jnp.where(column < PG * PAGE, n * PAGE, token + (PG * PAGE + 1))
        scores = jnp.where(column < limit, scores, -1e30)
        highest = jnp.max(scores, axis=1, keepdims=True)
        weights = jnp.exp(scores - highest)
        total = jnp.sum(weights, axis=1, keepdims=True)
        out = jnp.dot(weights.astype(jnp.bfloat16), kv[:, HS:kvw], preferred_element_type=jnp.float32)
        out = (out / total).astype(jnp.bfloat16)
        span = pl.ds(pl.multiple_of(j * PAGE, PAGE), PAGE)
        for h in range(heads):
            attnv[span, h * HS : (h + 1) * HS] = out[h * PAGE : (h + 1) * PAGE]
        return 0

    lax.fori_loop(0, requests, attend, 0)

    meta_copy.wait()
    for p in range(EARLY):
        arrived_tp(copy_za(p))
        own_za[p].wait()
    arrived_grp(copy_b)
    own_b.wait()

    def place(who):
        for k in range(PAIR):
            slot = PAIR * who + k
            n = metas[who, k, 0]
            page = fresh[slot]
            for p in range(PG):
                pages[slot, p] = jnp.where(n == p, page, pages[slot, p])
            pages[slot, PG] = jnp.where(n == PG, page, jnp.zeros_like(page))

    sent_tp(copy_zb)
    for p in range(EARLY):
        sent_grp(copy_a(p))
        sent_tp(copy_za(p))
    sent_grp(copy_m)
    sent_tp(copy_zn)
    sent_grp(copy_b)
    own_n.wait()
    place(g)
    for i in range(1, GRP):
        who = grp_back(g, i)
        copy_n(i, who).wait_recv()
        place(who)
    sent_grp(copy_n)


def out_kernel(attnv, pagesv, attn, pages, sems):
    rows, slots = attnv.shape[0], pagesv.shape[0]
    copies = []
    for i in range(slots // 4):
        part = pl.ds(i * 4, 4)
        copies.append(pltpu.make_async_copy(pagesv.at[part], pages.at[part], sems.at[i]))
    for i in range(2):
        part = pl.ds(i * (rows // 2), rows // 2)
        copies.append(
            pltpu.make_async_copy(attnv.at[part], attn.at[part], sems.at[slots // 4 + i])
        )
    for copy in copies:
        copy.start()
    for copy in copies:
        copy.wait()


def local(
    hidden, norm_gain, w_query, b_query, w_key, b_key, w_value, b_value,
    kv_pool, page_table, prefix_len, request_group,
):
    rows, width = hidden.shape
    qw = w_query.shape[1]
    requests = prefix_len.shape[0]
    npool = kv_pool.shape[0]
    kvw = kv_pool.shape[2]
    page_rows = PAGE // TP
    full = TP * kvw
    slots = PAIR * GRP
    bf = jnp.bfloat16
    cosine, sine = rope_tables()
    any_ = pl.BlockSpec(memory_space=pl.ANY)
    vmem = pl.BlockSpec(memory_space=pltpu.VMEM)
    dma = pltpu.SemaphoreType.DMA
    attn, pages = pl.pallas_call(
        main_kernel,
        name="span_and_routes",
        out_shape=[
            pltpu.VMEM((rows, qw), bf),
            pltpu.VMEM((slots, PG + 1, page_rows, full), bf),
        ],
        in_specs=[any_] * 14,
        out_specs=[vmem, vmem],
        scratch_shapes=[
            pltpu.VMEM((rows, width), bf),
            pltpu.VMEM((width, qw), bf),
            pltpu.VMEM((width, 2 * HS), bf),
            pltpu.VMEM((npool, TP, page_rows, kvw), bf),
            pltpu.VMEM((rows, HS), jnp.float32),
            pltpu.VMEM((RB, qw), jnp.float32),
            pltpu.VMEM((requests, PAGE, kvw), bf),
            pltpu.VMEM((requests, qw // HS * PAGE, HS), bf),
            pltpu.VMEM((slots, page_rows, full), bf),
            pltpu.VMEM((GRP, 8, 128), jnp.int32),
            pltpu.SMEM((GRP, 8, 128), jnp.int32),
            pltpu.VMEM((16, width), bf),
            pltpu.VMEM((EARLY, slots, TP, page_rows, kvw), bf),
            pltpu.VMEM((EARLY, slots, TP, page_rows, kvw), bf),
            pltpu.VMEM(((PG - EARLY) * requests, TP, page_rows, kvw), bf),
            pltpu.VMEM(((PG - EARLY) * requests, page_rows, full), bf),
            pltpu.VMEM((requests, TP, page_rows, kvw), bf),
            pltpu.VMEM((requests, page_rows, full), bf),
            pltpu.VMEM((slots, PG - EARLY, page_rows, full), bf),
            pltpu.VMEM((slots, page_rows, full), bf),
            pltpu.VMEM((GRP, 8, 128), jnp.int32),
            pltpu.SMEM((slots,), jnp.int32),
            pltpu.VMEM((width // HS, HS), bf),
            pltpu.VMEM((qw // HS, HS), bf),
            pltpu.VMEM((1, HS), bf),
            pltpu.VMEM((1, HS), bf),
            pltpu.VMEM(cosine.shape, jnp.float32),
            pltpu.VMEM(sine.shape, jnp.float32),
            pltpu.SMEM((PG, requests), jnp.int32),
            pltpu.SMEM((requests,), jnp.int32),
            pltpu.SMEM((request_group.shape[0],), jnp.int32),
            dma((9,)),
            dma((4 + rows // RB,)),
            dma((8 + EARLY,)),
            dma((EARLY, GRP)), dma((EARLY, GRP)),
            dma((GRP,)), dma((GRP,)),
            dma((GRP,)), dma((GRP,)),
            dma((GRP,)), dma((GRP,)),
            dma((EARLY, TP)), dma((EARLY, TP)),
            dma((TP,)), dma((TP,)),
            dma((TP,)), dma((TP,)),
        ],
        cost_estimate=pl.CostEstimate(
            flops=2 * rows * width * (qw + 2 * HS), bytes_accessed=40 << 20, transcendentals=0
        ),
        compiler_params=pltpu.CompilerParams(
            collective_id=0, has_side_effects=True, vmem_limit_bytes=58 << 20
        ),
    )(
        hidden,
        norm_gain.reshape(width // HS, HS),
        w_query,
        b_query.reshape(qw // HS, HS),
        w_key,
        b_key.reshape(1, HS),
        w_value,
        b_value.reshape(1, HS),
        kv_pool.reshape(npool, TP, page_rows, kvw),
        jnp.asarray(cosine),
        jnp.asarray(sine),
        page_table.T,
        prefix_len,
        request_group.reshape(-1),
    )
    attn, pages = pl.pallas_call(
        out_kernel,
        name="write_out",
        out_shape=[
            jax.ShapeDtypeStruct(attn.shape, bf),
            jax.ShapeDtypeStruct(pages.shape, bf),
        ],
        in_specs=[vmem, vmem],
        out_specs=[any_, any_],
        scratch_shapes=[dma((2 + slots // 4,))],
        compiler_params=pltpu.CompilerParams(vmem_limit_bytes=1 << 20),
    )(attn, pages)
    return attn, pages.reshape(slots * (PG + 1), page_rows, full)


def solution(mesh):
    in_specs = (
        P("grp", None),
        P(),
        P(None, "tp"),
        P("tp"),
        P(None, "tp"),
        P("tp"),
        P(None, "tp"),
        P("tp"),
        P("grp", None, "tp"),
        P("grp", None),
        P("grp"),
        P(),
    )
    out_specs = (P("grp", "tp"), P("grp", "tp", None))
    return jax.shard_map(local, mesh=mesh, in_specs=in_specs, out_specs=out_specs, check_vma=False)
```
